32 devices in a mesh: grp: 2 (over y), page: 4 (over z), tp: 2 (over x), sub: 2 (over core).
Axes of the slice: x: 2, y: 2, z: 4, core: 2. Of those that a mesh axis runs over, the one named last changes fastest.
Arguments:
- tokens: bfloat16 [4096, 8192], P(('grp', 'page'), ('tp', 'sub')), parts along dimension 0, may hold values from -6 to 6
- base_value_weight: bfloat16 [8192, 1024], P(('tp', 'sub')), may hold values from -0.0625 to 0.0625
- adapter_down_weight: bfloat16 [16384, 1024], P(('grp', 'tp', 'sub'), 'page'), parts along dimension 0, may hold values from -0.0625 to 0.0625
- adapter_up_weight: bfloat16 [2048, 1024], P(('grp', 'page'), ('tp', 'sub')), parts along dimension 0, may hold values from -0.75 to 0.75
- row_adapter_index: int32 [4096], P(('grp', 'page')), parts along dimension 0, may hold values from 0 to 15, as said below
- adapter_storage_slot: int32 [32], P('grp'), parts along dimension 0, may hold values from 0 to 15, as said below
Outputs:
- values: bfloat16 [4096, 1024], P(('grp', 'page'), ('tp', 'sub')), parts along dimension 0
The draws below stay inside these ranges and needn't reach their ends.
There are 2 independent parts, one for each index of `grp`. The reference program is written for one: setup_inputs(seed, part) draws one part's arguments, and reference() takes and returns one part's arrays. A program takes and returns all parts, laid end to end along the dimension named above; an argument that names none is the same for every part. Nothing has to cross between parts.
Inputs may be any that keep to these rules, and one draw needn't show every extreme that they name: `adapter_storage_slot`: adapter ids are the slots in some order: every value occurs once. `row_adapter_index`: of the 512 rows of one index of page, at most 256 have adapters whose slots lie in one page, and at most 384 have adapters whose slots lie in page j or page j + 2; in every draw one page receives exactly 256 rows and that pair of pages exactly 384 rows from every index of page.
All inputs are finite; a program needn't handle non-finite values.
Results may differ from the reference program's by a relative error of at most 0.0037.
Values may be sent and summed in bfloat16 or wider, within the bound.
A program may use at most 64 MiB of HBM per device.

```python
import jax
import jax.numpy as jnp
from jax import lax

MODEL_WIDTH = 8192
VALUE_WIDTH = 1024
ADAPTER_RANK = 64
ROW_DEV = 512
ADP_PAGE = 4
ADAPTER_TOTAL = 16
DECODE_ROWS = 2048
CAP = 256


def shared_layout(key):
    perm = jax.random.permutation(jax.random.fold_in(key, 11), ADAPTER_TOTAL).astype(jnp.int32)
    devices = DECODE_ROWS // ROW_DEV
    adapter_pages = ADAPTER_TOTAL // ADP_PAGE
    mean_rows = ROW_DEV // adapter_pages
    hottest = jax.random.randint(jax.random.fold_in(key, 12), (), 0, adapter_pages).astype(jnp.int32)
    partner = (hottest + adapter_pages // 2) % adapter_pages
    lower = jnp.minimum(hottest, partner)
    upper = jnp.maximum(hottest, partner)
    device_keys = jax.random.split(jax.random.fold_in(key, 13), devices)

    def one_device(dkey):
        key_a, key_b, key_c = jax.random.split(dkey, 3)
        others = jax.random.permutation(key_a, adapter_pages - 2).astype(jnp.int32)
        others = others + (others >= lower).astype(jnp.int32)
        others = others + (others >= upper).astype(jnp.int32)
        places = jnp.arange(ROW_DEV, dtype=jnp.int32)
        spot = jnp.maximum(places - CAP - mean_rows, 0) % (adapter_pages - 2)
        page_of = jnp.where(places < CAP, hottest, jnp.where(places < CAP + mean_rows, partner, others[spot]))
        page_of = jax.random.permutation(key_b, page_of)
        within = jax.random.randint(key_c, (ROW_DEV,), 0, ADP_PAGE).astype(jnp.int32)
        return page_of * ADP_PAGE + within
    slots = jax.vmap(one_device)(device_keys).reshape(DECODE_ROWS)
    owner_of = jnp.argsort(perm).astype(jnp.int32)
    return (perm, owner_of[slots].astype(jnp.int32))


def draw_adapter_storage_slot(key, part):
    return shared_layout(key)[0]


def draw_row_adapter_index(key, part):
    return shared_layout(key)[1]


def steps_of(rng, shape, shards, least, top_value):
    level = 1.0
    for position, blocks in shards:
        heights = jax.random.uniform(jax.random.fold_in(jax.random.fold_in(rng, 6), position), (blocks,), jnp.float32, least / len(shards), top_value / len(shards))
        level = level * jnp.repeat(jnp.exp(heights), shape[position] // blocks).reshape((-1,) + (1,) * (len(shape) - 1 - position))
    return level


def normal_values(key, dims, deviation, bound, pieces=(), held_as=jnp.bfloat16):
    loudness = steps_of(key, dims, pieces, -0.22, 0.18) if pieces else 1.0
    entries = jax.random.normal(key, dims, jnp.float32) * deviation * loudness
    return jnp.minimum(jnp.maximum(entries, -bound), bound).astype(held_as)


def setup_inputs(seed: int = 0, part: int = 0) -> dict:
    key_of = jax.random.split(jax.random.key(seed), 7)
    own_keys = jax.random.split(jax.random.fold_in(key_of[6], part), 7)
    tokens = normal_values(own_keys[0], (DECODE_ROWS, MODEL_WIDTH), 1.0, 6.0, ((0, 4), (1, 4)))
    base_value_weight = normal_values(key_of[1], (MODEL_WIDTH, VALUE_WIDTH), MODEL_WIDTH ** -0.5, 0.0625, ((0, 4),))
    adapter_down_weight = normal_values(own_keys[2], (MODEL_WIDTH, ADAPTER_TOTAL * ADAPTER_RANK), MODEL_WIDTH ** -0.5, 0.0625, ((0, 4), (1, 4)))
    adapter_up_weight = normal_values(own_keys[3], (ADAPTER_TOTAL * ADAPTER_RANK, VALUE_WIDTH), ADAPTER_RANK ** -0.5, 0.75, ((0, 4), (1, 4)))
    row_adapter_index = draw_row_adapter_index(jax.random.fold_in(jax.random.fold_in(key_of[6], part), 71), part)
    adapter_storage_slot = draw_adapter_storage_slot(jax.random.fold_in(jax.random.fold_in(key_of[6], part), 71), part)
    return dict(tokens=tokens, base_value_weight=base_value_weight, adapter_down_weight=adapter_down_weight, adapter_up_weight=adapter_up_weight, row_adapter_index=row_adapter_index, adapter_storage_slot=adapter_storage_slot)


adapter_scale = 0.5


def reference(tokens, base_value_weight, adapter_down_weight, adapter_up_weight, row_adapter_index, adapter_storage_slot):
    storage_position = adapter_storage_slot[row_adapter_index].astype(jnp.int32)
    base_output = jnp.dot(tokens, base_value_weight, preferred_element_type=jnp.float32)
    down_weight_cube = adapter_down_weight.reshape(MODEL_WIDTH, ADAPTER_TOTAL, ADAPTER_RANK)
    up_weight_cube = adapter_up_weight.reshape(ADAPTER_TOTAL, ADAPTER_RANK, VALUE_WIDTH)

    def single_block(pair):
        rows, slots = pair
        down_rows = jnp.take(down_weight_cube, slots, axis=1).astype(jnp.float32)
        shrink_rank = jnp.einsum("bd,dbr->br", rows.astype(jnp.float32), down_rows).astype(jnp.bfloat16)
        up_weight_rows = up_weight_cube[slots].astype(jnp.float32)
        expand_rank = jnp.einsum("cn,cnm->cm", shrink_rank.astype(jnp.float32), up_weight_rows) * adapter_scale
        return expand_rank.astype(jnp.bfloat16)

    adapter_output = lax.map(single_block, (tokens.reshape(-1, 32, MODEL_WIDTH), storage_position.reshape(-1, 32)))
    adapter_output = adapter_output.reshape(DECODE_ROWS, VALUE_WIDTH)
    return (base_output + adapter_output.astype(jnp.float32)).astype(jnp.bfloat16)
```

```python
import functools

import jax
import jax.numpy as jnp
from jax import lax
from jax.experimental import pallas as pl
from jax.experimental.pallas import tpu as pltpu
from jax.sharding import PartitionSpec as P

ADAPTER_RANK = 64


adapter_scale = 0.5


def rank_within(labels, count):
    onehot = (labels[:, None] == jnp.arange(count, dtype=jnp.int32)[None, :]).astype(jnp.int32)
    before = jnp.cumsum(onehot, axis=0) - onehot
    return jnp.sum(before * onehot, axis=1)


def build_device_worker(down_cols, up_weight_rows):
    width = down_cols.shape[1]
    row_grouping = width // ADAPTER_RANK
    column_group = jnp.arange(width, dtype=jnp.int32) // ADAPTER_RANK

    def owner_work(pair):
        rows, marks = pair
        sources = marks.shape[0]
        count = marks.shape[1]
        feat = rows.shape[2]
        flat_rows = rows.reshape(sources * count, feat)
        owner_ids = marks.reshape(sources * count).astype(jnp.int32)
        select = owner_ids[:, None] == column_group[None, :]
        partial_all = jnp.dot(flat_rows, down_cols, preferred_element_type=jnp.float32)
        picked = (
            jnp.where(select, partial_all, 0.0)
            .reshape(sources * count, row_grouping, ADAPTER_RANK)
            .sum(axis=1)
        )
        shrink_rank = lax.psum(picked, ("tp", "sub")).astype(jnp.bfloat16)
        spread_rows = jnp.where(
            select, jnp.tile(shrink_rank, (1, row_grouping)), jnp.zeros((), jnp.bfloat16)
        )
        expand_rank = (
            jnp.dot(spread_rows, up_weight_rows, preferred_element_type=jnp.float32) * adapter_scale
        )
        return expand_rank.astype(jnp.bfloat16).reshape(sources, count, expand_rank.shape[1])

    return owner_work


def pack_boxes(tokens, flattened, marks, adapter_pages, slot_capacity):
    feat = tokens.shape[1]
    outbox = (
        jnp.zeros((adapter_pages * slot_capacity, feat), jnp.bfloat16).at[flattened].set(tokens)
    )
    labels = (
        jnp.full((adapter_pages * slot_capacity,), -1.0, jnp.bfloat16)
        .at[flattened]
        .set(marks.astype(jnp.bfloat16))
    )
    return (
        outbox.reshape(adapter_pages, slot_capacity, feat),
        labels.reshape(adapter_pages, slot_capacity),
    )


def exchange_rows_body(
    tokens,
    base_value_weight,
    adapter_down_weight,
    adapter_up_weight,
    row_adapter_index,
    adapter_storage_slot,
):
    adapter_pages = lax.axis_size("page")
    row_dev = tokens.shape[0]
    slot_capacity = min(4 * row_dev // adapter_pages, row_dev // 2)
    row_grouping = adapter_down_weight.shape[1] // ADAPTER_RANK
    hits = (
        row_adapter_index[:, None]
        == jnp.arange(adapter_storage_slot.shape[0], dtype=jnp.int32)[None, :]
    )
    storage_position = jnp.sum(jnp.where(hits, adapter_storage_slot[None, :], 0), axis=1)
    target = storage_position // row_grouping
    within = storage_position % row_grouping
    position = rank_within(target, adapter_pages)
    flattened = target * slot_capacity + position
    outbox, labels = pack_boxes(tokens, flattened, within, adapter_pages, slot_capacity)
    device_worker = build_device_worker(adapter_down_weight, adapter_up_weight)
    finished = device_worker(
        (
            lax.all_to_all(outbox, "page", split_axis=0, concat_axis=0, tiled=True),
            lax.all_to_all(labels, "page", split_axis=0, concat_axis=0, tiled=True),
        )
    )
    returned_output = lax.all_to_all(finished, "page", split_axis=0, concat_axis=0, tiled=True)
    adapter_row_output = returned_output.reshape(
        adapter_pages * slot_capacity, returned_output.shape[2]
    )[flattened]
    partial_base = jnp.dot(tokens, base_value_weight, preferred_element_type=jnp.float32)
    base_output_share = lax.psum_scatter(
        partial_base, ("tp", "sub"), scatter_dimension=1, tiled=True
    )
    return (base_output_share + adapter_row_output.astype(jnp.float32)).astype(jnp.bfloat16)


MESH_ID = pl.DeviceIdType.MESH
CHUNKS = 2


def page_in_turn(z, turn, n):
    if turn == 0:
        return z
    nearer = jnp.minimum(z, n - 1 - z)
    step = -((turn + 1) // 2) if turn % 2 else turn // 2
    beyond = jnp.where(z < n - 1 - z, z + (turn - nearer), z - (turn - nearer))
    return jnp.where(turn <= 2 * nearer, z + step, beyond)


def gather_kernel(
    n,
    adapters,
    tokens_hbm,
    base_hbm,
    down_hbm,
    up_hbm,
    index_ref,
    slot_ref,
    out_ref,
    tok,
    basew,
    down_all,
    up_all,
    part,
    picked,
    near_base,
    far_base,
    shrink_send,
    near_shrink,
    far_send,
    far_shrink,
    load_sem,
    right_sem,
    left_sem,
    recv_sem,
    sum_send_sem,
    sum_recv_sem,
):
    z, t, s = lax.axis_index("page"), lax.axis_index("tp"), lax.axis_index("sub")
    rows, depth = tok.shape
    rank = ADAPTER_RANK
    group = down_all.shape[2] // rank
    piece = depth // CHUNKS

    loads = [
        pltpu.make_async_copy(down_hbm, down_all.at[z], load_sem.at[0]),
        pltpu.make_async_copy(up_hbm, up_all.at[z], load_sem.at[1]),
        pltpu.make_async_copy(tokens_hbm, tok, load_sem.at[2]),
        pltpu.make_async_copy(base_hbm, basew, load_sem.at[3]),
    ]
    for load in loads:
        load.start()

    barrier = pltpu.get_barrier_semaphore()
    pl.semaphore_signal(barrier, inc=1, device_id={"tp": 1 - t}, device_id_type=MESH_ID)
    pl.semaphore_signal(barrier, inc=1, device_id={"sub": 1 - s}, device_id_type=MESH_ID)

    @pl.when(z > 0)
    def _():
        pl.semaphore_signal(barrier, inc=1, device_id={"page": z - 1}, device_id_type=MESH_ID)

    @pl.when(z < n - 1)
    def _():
        pl.semaphore_signal(barrier, inc=1, device_id={"page": z + 1}, device_id_type=MESH_ID)

    pl.semaphore_wait(barrier, 2 + (z > 0).astype(jnp.int32) + (z < n - 1).astype(jnp.int32))

    def hop(page, chunk, to, sems):
        if chunk < CHUNKS:
            ref = down_all.at[page, pl.ds(chunk * piece, piece), :]
        else:
            ref = up_all.at[page]
        return pltpu.make_async_remote_copy(
            src_ref=ref,
            dst_ref=ref,
            send_sem=sems.at[page, chunk],
            recv_sem=recv_sem.at[page, chunk],
            device_id={"page": to},
            device_id_type=MESH_ID,
        )

    def send_on(page, chunk):
        @pl.when((page <= z) & (z < n - 1))
        def _():
            hop(page, chunk, z + 1, right_sem).start()

        @pl.when((page >= z) & (z > 0))
        def _():
            hop(page, chunk, z - 1, left_sem).start()

    loads[0].wait()
    for chunk in range(CHUNKS):
        send_on(z, chunk)
    loads[1].wait()
    send_on(z, CHUNKS)

    slot_row = jnp.zeros(index_ref.shape, jnp.float32)
    for a in range(adapters):
        slot_row = jnp.where(index_ref[...] == a, slot_ref[a].astype(jnp.float32), slot_row)
    slot = jnp.transpose(jnp.broadcast_to(slot_row, (128, rows)))
    lane = lax.broadcasted_iota(jnp.int32, (rows, 128), 1)
    half = (lane // rank).astype(jnp.float32)
    loads[2].wait()
    loads[3].wait()
    blocks, width = part.shape[0], part.shape[2]

    @pl.loop(0, blocks)
    def _(b):
        columns = pl.ds(pl.multiple_of(b * width, width), width)
        part[b] = jnp.dot(tok[...], basew[:, columns], preferred_element_type=jnp.float32)

    def to_sibling(k):
        return pltpu.make_async_remote_copy(
            src_ref=part.at[2 * k + 1 - s],
            dst_ref=near_base.at[k],
            send_sem=sum_send_sem.at[k],
            recv_sem=sum_recv_sem.at[k],
            device_id={"sub": 1 - s},
            device_id_type=MESH_ID,
        )

    base_far = pltpu.make_async_remote_copy(
        src_ref=part.at[2 * (1 - t) + s],
        dst_ref=far_base,
        send_sem=sum_send_sem.at[2],
        recv_sem=sum_recv_sem.at[2],
        device_id={"tp": 1 - t},
        device_id_type=MESH_ID,
    )
    for k in range(2):
        to_sibling(k).start()

    def pick(page, product):
        first = (page * group).astype(jnp.float32) + half
        total = jnp.zeros((rows, 128), jnp.float32)
        for g in range(group * rank // 128):
            hit = slot == first + float(g * (128 // rank))
            total += jnp.where(hit, product[:, g * 128 : g * 128 + 128], 0.0)
        return total

    for turn in range(n):
        page = page_in_turn(z, turn, n)
        for chunk in range(CHUNKS):
            if turn:
                hop(page, chunk, z, left_sem).wait_recv()
                send_on(page, chunk)
            span = pl.ds(chunk * piece, piece)
            product = jnp.dot(
                tok[:, chunk * piece : chunk * piece + piece],
                down_all[page, span, :],
                preferred_element_type=jnp.float32,
            )
            if turn == 0 and chunk == 0:
                picked[...] = pick(page, product)
            else:
                picked[...] += pick(page, product)
        if turn:
            hop(page, CHUNKS, z, left_sem).wait_recv()
            send_on(page, CHUNKS)
        if turn == 0:
            for k in range(2):
                to_sibling(k).wait_recv()
            part[2 * (1 - t) + s] += near_base[1 - t]
            base_far.start()

    folded = picked[...] + pltpu.roll(picked[...], rank, 1)
    low = lane[: rows // 2] < rank
    shrink_send[...] = jnp.where(low, folded[: rows // 2], folded[rows // 2 :])
    near = pltpu.make_async_remote_copy(
        src_ref=shrink_send,
        dst_ref=near_shrink,
        send_sem=sum_send_sem.at[3],
        recv_sem=sum_recv_sem.at[3],
        device_id={"sub": 1 - s},
        device_id_type=MESH_ID,
    )
    near.start()
    near.wait_recv()
    far_send[...] = shrink_send[...] + near_shrink[...]
    far = pltpu.make_async_remote_copy(
        src_ref=far_send,
        dst_ref=far_shrink,
        send_sem=sum_send_sem.at[4],
        recv_sem=sum_recv_sem.at[4],
        device_id={"tp": 1 - t},
        device_id_type=MESH_ID,
    )
    far.start()
    base_far.wait_recv()
    part[2 * t + s] += near_base[t] + far_base[...]
    far.wait_recv()
    both = far_send[...] + far_shrink[...]
    both = both.astype(jnp.bfloat16).astype(jnp.float32)
    turned = pltpu.roll(both, rank, 1)
    shrink = jnp.concatenate(
        [jnp.where(low, both, turned), jnp.where(low, turned, both)], axis=0
    )
    spread = jnp.concatenate(
        [
            jnp.where(slot == half + float(b * (128 // rank)), shrink, 0.0).astype(jnp.bfloat16)
            for b in range(n * group * rank // 128)
        ],
        axis=1,
    )
    expand = jnp.dot(
        spread,
        up_all[...].reshape(n * group * rank, up_all.shape[2]),
        preferred_element_type=jnp.float32,
    )
    lora = (expand * adapter_scale).astype(jnp.bfloat16).astype(jnp.float32)
    out_ref[...] = (part[2 * t + s] + lora).astype(jnp.bfloat16)

    for k in range(2):
        to_sibling(k).wait_send()
    base_far.wait_send()
    near.wait_send()
    far.wait_send()
    for turn in range(n):
        page = page_in_turn(z, turn, n)
        for chunk in range(CHUNKS + 1):

            @pl.when((page <= z) & (z < n - 1))
            def _():
                hop(page, chunk, z + 1, right_sem).wait_send()

            @pl.when((page >= z) & (z > 0))
            def _():
                hop(page, chunk, z - 1, left_sem).wait_send()


def gather_weights_body(
    tokens,
    base_value_weight,
    adapter_down_weight,
    adapter_up_weight,
    row_adapter_index,
    adapter_storage_slot,
):
    n = lax.axis_size("page")
    rows, depth = tokens.shape
    width = adapter_down_weight.shape[1]
    share = adapter_up_weight.shape[1]
    blocks = base_value_weight.shape[1] // share
    adapters = adapter_storage_slot.shape[0]
    f32, bf16 = jnp.float32, jnp.bfloat16
    return pl.pallas_call(
        functools.partial(gather_kernel, n, adapters),
        out_shape=jax.ShapeDtypeStruct((rows, share), bf16),
        in_specs=[pl.BlockSpec(memory_space=pl.ANY)] * 4
        + [
            pl.BlockSpec(memory_space=pltpu.VMEM),
            pl.BlockSpec(memory_space=pltpu.SMEM),
        ],
        out_specs=pl.BlockSpec(memory_space=pltpu.VMEM),
        scratch_shapes=[
            pltpu.VMEM((rows, depth), bf16),
            pltpu.VMEM(base_value_weight.shape, bf16),
            pltpu.VMEM((n, depth, width), bf16),
            pltpu.VMEM((n, width, share), bf16),
            pltpu.VMEM((blocks, rows, share), f32),
            pltpu.VMEM((rows, 128), f32),
            pltpu.VMEM((2, rows, share), f32),
            pltpu.VMEM((rows, share), f32),
            pltpu.VMEM((rows // 2, 128), f32),
            pltpu.VMEM((rows // 2, 128), f32),
            pltpu.VMEM((rows // 2, 128), f32),
            pltpu.VMEM((rows // 2, 128), f32),
            pltpu.SemaphoreType.DMA((4,)),
            pltpu.SemaphoreType.DMA((n, CHUNKS + 1)),
            pltpu.SemaphoreType.DMA((n, CHUNKS + 1)),
            pltpu.SemaphoreType.DMA((n, CHUNKS + 1)),
            pltpu.SemaphoreType.DMA((5,)),
            pltpu.SemaphoreType.DMA((5,)),
        ],
        compiler_params=pltpu.CompilerParams(
            collective_id=0, has_side_effects=True, vmem_limit_bytes=48 * 1024 * 1024
        ),
    )(
        tokens,
        base_value_weight,
        adapter_down_weight,
        adapter_up_weight,
        row_adapter_index.reshape(1, rows),
        adapter_storage_slot,
    )


def solution(mesh):
    sizes = mesh.shape
    gathers = sizes["page"] <= 4 and sizes["tp"] == 2 and sizes["sub"] == 2
    return jax.shard_map(
        gather_weights_body if gathers else exchange_rows_body,
        mesh=mesh,
        in_specs=(
            P(("grp", "page"), ("tp", "sub")),
            P(("tp", "sub"), None),
            P(("grp", "tp", "sub"), "page"),
            P(("grp", "page"), ("tp", "sub")),
            P(("grp", "page")),
            P("grp"),
        ),
        out_specs=P(("grp", "page"), ("tp", "sub")),
        check_vma=False,
    )
```

```python
import functools

import jax
import jax.numpy as jnp
from jax import lax
from jax.experimental import pallas as pl
from jax.experimental.pallas import tpu as pltpu
from jax.sharding import PartitionSpec as P

ADAPTER_RANK = 64


adapter_scale = 0.5


def rank_within(labels, count):
    onehot = (labels[:, None] == jnp.arange(count, dtype=jnp.int32)[None, :]).astype(jnp.int32)
    before = jnp.cumsum(onehot, axis=0) - onehot
    return jnp.sum(before * onehot, axis=1)


def build_device_worker(down_cols, up_weight_rows):
    width = down_cols.shape[1]
    row_grouping = width // ADAPTER_RANK
    column_group = jnp.arange(width, dtype=jnp.int32) // ADAPTER_RANK

    def owner_work(pair):
        rows, marks = pair
        sources = marks.shape[0]
        count = marks.shape[1]
        feat = rows.shape[2]
        flat_rows = rows.reshape(sources * count, feat)
        owner_ids = marks.reshape(sources * count).astype(jnp.int32)
        select = owner_ids[:, None] == column_group[None, :]
        partial_all = jnp.dot(flat_rows, down_cols, preferred_element_type=jnp.float32)
        picked = (
            jnp.where(select, partial_all, 0.0)
            .reshape(sources * count, row_grouping, ADAPTER_RANK)
            .sum(axis=1)
        )
        shrink_rank = lax.psum(picked, ("tp", "sub")).astype(jnp.bfloat16)
        spread_rows = jnp.where(
            select, jnp.tile(shrink_rank, (1, row_grouping)), jnp.zeros((), jnp.bfloat16)
        )
        expand_rank = (
            jnp.dot(spread_rows, up_weight_rows, preferred_element_type=jnp.float32) * adapter_scale
        )
        return expand_rank.astype(jnp.bfloat16).reshape(sources, count, expand_rank.shape[1])

    return owner_work


def pack_boxes(tokens, flattened, marks, adapter_pages, slot_capacity):
    feat = tokens.shape[1]
    outbox = (
        jnp.zeros((adapter_pages * slot_capacity, feat), jnp.bfloat16).at[flattened].set(tokens)
    )
    labels = (
        jnp.full((adapter_pages * slot_capacity,), -1.0, jnp.bfloat16)
        .at[flattened]
        .set(marks.astype(jnp.bfloat16))
    )
    return (
        outbox.reshape(adapter_pages, slot_capacity, feat),
        labels.reshape(adapter_pages, slot_capacity),
    )


def exchange_rows_body(
    tokens,
    base_value_weight,
    adapter_down_weight,
    adapter_up_weight,
    row_adapter_index,
    adapter_storage_slot,
):
    adapter_pages = lax.axis_size("page")
    row_dev = tokens.shape[0]
    slot_capacity = min(4 * row_dev // adapter_pages, row_dev // 2)
    row_grouping = adapter_down_weight.shape[1] // ADAPTER_RANK
    hits = (
        row_adapter_index[:, None]
        == jnp.arange(adapter_storage_slot.shape[0], dtype=jnp.int32)[None, :]
    )
    storage_position = jnp.sum(jnp.where(hits, adapter_storage_slot[None, :], 0), axis=1)
    target = storage_position // row_grouping
    within = storage_position % row_grouping
    position = rank_within(target, adapter_pages)
    flattened = target * slot_capacity + position
    outbox, labels = pack_boxes(tokens, flattened, within, adapter_pages, slot_capacity)
    device_worker = build_device_worker(adapter_down_weight, adapter_up_weight)
    finished = device_worker(
        (
            lax.all_to_all(outbox, "page", split_axis=0, concat_axis=0, tiled=True),
            lax.all_to_all(labels, "page", split_axis=0, concat_axis=0, tiled=True),
        )
    )
    returned_output = lax.all_to_all(finished, "page", split_axis=0, concat_axis=0, tiled=True)
    adapter_row_output = returned_output.reshape(
        adapter_pages * slot_capacity, returned_output.shape[2]
    )[flattened]
    partial_base = jnp.dot(tokens, base_value_weight, preferred_element_type=jnp.float32)
    base_output_share = lax.psum_scatter(
        partial_base, ("tp", "sub"), scatter_dimension=1, tiled=True
    )
    return (base_output_share + adapter_row_output.astype(jnp.float32)).astype(jnp.bfloat16)


MESH_ID = pl.DeviceIdType.MESH
CHUNKS = 2


def page_in_turn(z, turn, n):
    if turn == 0:
        return z
    nearer = jnp.minimum(z, n - 1 - z)
    step = -((turn + 1) // 2) if turn % 2 else turn // 2
    beyond = jnp.where(z < n - 1 - z, z + (turn - nearer), z - (turn - nearer))
    return jnp.where(turn <= 2 * nearer, z + step, beyond)


def gather_kernel(
    n,
    adapters,
    tokens_hbm,
    base_hbm,
    down_hbm,
    up_hbm,
    index_hbm,
    slot_hbm,
    out_ref,
    index_ref,
    slot_ref,
    tok,
    basew,
    down_all,
    up_all,
    pack,
    pack_slot,
    place,
    pack_send,
    pack_back,
    part,
    picked,
    near_base,
    far_base,
    shrink_send,
    near_shrink,
    far_send,
    far_shrink,
    load_sem,
    right_sem,
    left_sem,
    recv_sem,
    pack_send_sem,
    pack_recv_sem,
    sum_send_sem,
    sum_recv_sem,
):
    z, t, s = lax.axis_index("page"), lax.axis_index("tp"), lax.axis_index("sub")
    rows, depth = tok.shape
    rank = ADAPTER_RANK
    group = down_all.shape[2] // rank
    piece = depth // CHUNKS

    loads = [
        pltpu.make_async_copy(down_hbm, down_all.at[z], load_sem.at[0]),
        pltpu.make_async_copy(up_hbm, up_all.at[z], load_sem.at[1]),
        pltpu.make_async_copy(tokens_hbm, tok, load_sem.at[2]),
        pltpu.make_async_copy(base_hbm, basew, load_sem.at[3]),
        pltpu.make_async_copy(index_hbm, index_ref, load_sem.at[4]),
        pltpu.make_async_copy(slot_hbm, slot_ref, load_sem.at[5]),
    ]
    for load in loads:
        load.start()

    barrier = pltpu.get_barrier_semaphore()
    pl.semaphore_signal(barrier, inc=1, device_id={"tp": 1 - t}, device_id_type=MESH_ID)
    pl.semaphore_signal(barrier, inc=1, device_id={"sub": 1 - s}, device_id_type=MESH_ID)

    @pl.when(z > 0)
    def _():
        pl.semaphore_signal(barrier, inc=1, device_id={"page": z - 1}, device_id_type=MESH_ID)

    @pl.when(z < n - 1)
    def _():
        pl.semaphore_signal(barrier, inc=1, device_id={"page": z + 1}, device_id_type=MESH_ID)

    pl.semaphore_wait(barrier, 2 + (z > 0).astype(jnp.int32) + (z < n - 1).astype(jnp.int32))

    end = (z == 0) | (z == n - 1)
    helped = jnp.where(z == 1, 0, n - 1)
    helper = jnp.where(z == 0, 1, n - 2)
    opposite = n - 1 - z

    def hop(page, chunk, to, sems, own=False):
        if chunk < CHUNKS:
            ref = down_all.at[page, pl.ds(chunk * piece, piece), :]
            src = down_hbm.at[pl.ds(chunk * piece, piece), :] if own else ref
        else:
            ref = up_all.at[page]
            src = up_hbm if own else ref
        return pltpu.make_async_remote_copy(
            src_ref=src,
            dst_ref=ref,
            send_sem=sems.at[page, chunk],
            recv_sem=recv_sem.at[page, chunk],
            device_id={"page": to},
            device_id_type=MESH_ID,
        )

    def goes_right(page, chunk):
        goes = (page <= z) & (z < n - 1)
        return goes & ~((z == n - 2) & (page == 0)) if chunk < CHUNKS else goes

    def goes_left(page, chunk):
        goes = (page >= z) & (z > 0)
        return goes & ~((z == 1) & (page == n - 1)) if chunk < CHUNKS else goes

    def send_on(page, chunk, own=False):
        @pl.when(goes_right(page, chunk))
        def _():
            hop(page, chunk, z + 1, right_sem, own).start()

        @pl.when(goes_left(page, chunk))
        def _():
            hop(page, chunk, z - 1, left_sem, own).start()

    for chunk in (CHUNKS, *range(CHUNKS)):
        send_on(z, chunk, own=True)

    def pack_copy(k, to):
        ref = (pack, pack_slot)[k]
        return pltpu.make_async_remote_copy(
            src_ref=ref,
            dst_ref=ref,
            send_sem=pack_send_sem.at[k],
            recv_sem=pack_recv_sem.at[k],
            device_id={"page": to},
            device_id_type=MESH_ID,
        )

    def pack_return(to):
        return pltpu.make_async_remote_copy(
            src_ref=pack_send,
            dst_ref=pack_back,
            send_sem=pack_send_sem.at[2],
            recv_sem=pack_recv_sem.at[2],
            device_id={"page": to},
            device_id_type=MESH_ID,
        )

    loads[4].wait()
    loads[5].wait()
    slot_row = jnp.zeros(index_ref.shape, jnp.float32)
    for a in range(adapters):
        slot_row = jnp.where(index_ref[...] == a, slot_ref[a].astype(jnp.float32), slot_row)
    slot = jnp.transpose(jnp.broadcast_to(slot_row, (128, rows)))
    lane = lax.broadcasted_iota(jnp.int32, (rows, 128), 1)
    half = (lane // rank).astype(jnp.float32)
    loads[2].wait()
    cap = pack.shape[0]

    @pl.when(end)
    def _():
        lowest = (opposite * group).astype(jnp.float32)
        mine = (slot_row >= lowest) & (slot_row < lowest + float(group))
        marks = jnp.broadcast_to(jnp.where(mine, 1.0, 0.0), (16, rows)).astype(jnp.bfloat16)
        earlier = lax.broadcasted_iota(jnp.int32, (rows, rows), 0) < lax.broadcasted_iota(
            jnp.int32, (rows, rows), 1
        )
        position = jnp.dot(
            marks,
            jnp.where(earlier, 1.0, 0.0).astype(jnp.bfloat16),
            preferred_element_type=jnp.float32,
        )[:1]
        target = jnp.where(mine, position, -1.0)
        spots = lax.broadcasted_iota(jnp.int32, (cap, rows), 0).astype(jnp.float32)
        place[...] = jnp.where(spots == target, 1.0, 0.0).astype(jnp.bfloat16)

        @pl.loop(0, depth // 512)
        def _(b):
            columns = pl.ds(pl.multiple_of(b * 512, 512), 512)
            pack[:, columns] = jnp.dot(
                place[...], tok[:, columns], preferred_element_type=jnp.float32
            ).astype(jnp.bfloat16)

        pack_slot[...] = lax.dot_general(
            jnp.broadcast_to(slot_row, (16, rows)).astype(jnp.bfloat16),
            place[...],
            (((1,), (1,)), ((), ())),
            preferred_element_type=jnp.float32,
        )[: pack_slot.shape[0]]
        for k in range(2):
            pack_copy(k, helper).start()

    loads[3].wait()
    blocks, width = part.shape[0], part.shape[2]

    @pl.loop(0, blocks)
    def _(b):
        columns = pl.ds(pl.multiple_of(b * width, width), width)
        part[b] = jnp.dot(tok[...], basew[:, columns], preferred_element_type=jnp.float32)

    def to_sibling(k):
        return pltpu.make_async_remote_copy(
            src_ref=part.at[2 * k + 1 - s],
            dst_ref=near_base.at[k],
            send_sem=sum_send_sem.at[k],
            recv_sem=sum_recv_sem.at[k],
            device_id={"sub": 1 - s},
            device_id_type=MESH_ID,
        )

    base_far = pltpu.make_async_remote_copy(
        src_ref=part.at[2 * (1 - t) + s],
        dst_ref=far_base,
        send_sem=sum_send_sem.at[2],
        recv_sem=sum_recv_sem.at[2],
        device_id={"tp": 1 - t},
        device_id_type=MESH_ID,
    )
    for k in range(2):
        to_sibling(k).start()

    def pick(page, product, slot, half):
        first = (page * group).astype(jnp.float32) + half
        total = jnp.zeros(slot.shape, jnp.float32)
        for g in range(group * rank // 128):
            hit = slot == first + float(g * (128 // rank))
            total += jnp.where(hit, product[:, g * 128 : g * 128 + 128], 0.0)
        return total

    def product_of(ref, page, chunk):
        return jnp.dot(
            ref[:, chunk * piece : chunk * piece + piece],
            down_all[page, pl.ds(chunk * piece, piece), :],
            preferred_element_type=jnp.float32,
        )

    def take_page(page, arrives):
        for chunk in range(CHUNKS):
            if arrives:
                hop(page, chunk, z, left_sem).wait_recv()
                send_on(page, chunk)
            picked[...] += pick(page, product_of(tok, page, chunk), slot, half)

    loads[0].wait()
    loads[1].wait()
    picked[...] = jnp.zeros_like(picked)
    take_page(z, False)
    for k in range(2):
        to_sibling(k).wait_recv()
    part[2 * (1 - t) + s] += near_base[1 - t]
    base_far.start()
    for turn in range(1, n - 1):
        page = page_in_turn(z, turn, n)
        hop(page, CHUNKS, z, left_sem).wait_recv()
        send_on(page, CHUNKS)
        take_page(page, True)

    last = page_in_turn(z, n - 1, n)
    hop(last, CHUNKS, z, left_sem).wait_recv()
    send_on(last, CHUNKS)

    @pl.when(~end)
    def _():
        for k in range(2):
            pack_copy(k, z).wait_recv()
        their_slot = jnp.transpose(jnp.broadcast_to(pack_slot[:1], (128, cap)))
        theirs = jnp.zeros((cap, 128), jnp.float32)
        for chunk in range(CHUNKS):
            hop(last, chunk, z, left_sem).wait_recv()
            send_on(last, chunk)
            theirs += pick(last, product_of(pack, last, chunk), their_slot, half[:cap])
        theirs += pltpu.roll(theirs, rank, 1)
        pack_send[...] = jnp.where(
            lane[: cap // 2] < rank, theirs[: cap // 2], theirs[cap // 2 :]
        ).astype(jnp.bfloat16)
        pack_return(helped).start()
        for chunk in range(CHUNKS):
            picked[...] += pick(last, product_of(tok, last, chunk), slot, half)

    @pl.when(end)
    def _():
        pack_return(z).wait_recv()
        back = pack_back[...].astype(jnp.float32)
        back = jnp.concatenate([back, pltpu.roll(back, rank, 1)], axis=0)
        back = jnp.where(lane[:cap] < rank, back, 0.0).astype(jnp.bfloat16)
        picked[...] += lax.dot_general(
            place[...], back, (((0,), (0,)), ((), ())), preferred_element_type=jnp.float32
        )

    folded = picked[...] + pltpu.roll(picked[...], rank, 1)
    low = lane[: rows // 2] < rank
    shrink_send[...] = jnp.where(low, folded[: rows // 2], folded[rows // 2 :])
    near = pltpu.make_async_remote_copy(
        src_ref=shrink_send,
        dst_ref=near_shrink,
        send_sem=sum_send_sem.at[3],
        recv_sem=sum_recv_sem.at[3],
        device_id={"sub": 1 - s},
        device_id_type=MESH_ID,
    )
    near.start()
    near.wait_recv()
    chip_sum = shrink_send[...] + near_shrink[...]
    far_send[...] = chip_sum.astype(jnp.bfloat16)
    far = pltpu.make_async_remote_copy(
        src_ref=far_send,
        dst_ref=far_shrink,
        send_sem=sum_send_sem.at[4],
        recv_sem=sum_recv_sem.at[4],
        device_id={"tp": 1 - t},
        device_id_type=MESH_ID,
    )
    far.start()
    base_far.wait_recv()
    part[2 * t + s] += near_base[t] + far_base[...]
    far.wait_recv()
    both = chip_sum + far_shrink[...].astype(jnp.float32)
    both = both.astype(jnp.bfloat16).astype(jnp.float32)
    turned = pltpu.roll(both, rank, 1)
    shrink = jnp.concatenate(
        [jnp.where(low, both, turned), jnp.where(low, turned, both)], axis=0
    )
    spread = jnp.concatenate(
        [
            jnp.where(slot == half + float(b * (128 // rank)), shrink, 0.0).astype(jnp.bfloat16)
            for b in range(n * group * rank // 128)
        ],
        axis=1,
    )
    expand = jnp.dot(
        spread,
        up_all[...].reshape(n * group * rank, up_all.shape[2]),
        preferred_element_type=jnp.float32,
    )
    lora = (expand * adapter_scale).astype(jnp.bfloat16).astype(jnp.float32)
    out_ref[...] = (part[2 * t + s] + lora).astype(jnp.bfloat16)

    for k in range(2):
        to_sibling(k).wait_send()
    base_far.wait_send()
    near.wait_send()
    far.wait_send()

    @pl.when(end)
    def _():
        for k in range(2):
            pack_copy(k, helper).wait_send()

    @pl.when(~end)
    def _():
        pack_return(helped).wait_send()

    for turn in range(n):
        page = page_in_turn(z, turn, n)
        for chunk in range(CHUNKS + 1):

            @pl.when(goes_right(page, chunk))
            def _():
                hop(page, chunk, z + 1, right_sem, turn == 0).wait_send()

            @pl.when(goes_left(page, chunk))
            def _():
                hop(page, chunk, z - 1, left_sem, turn == 0).wait_send()


def gather_weights_body(
    tokens,
    base_value_weight,
    adapter_down_weight,
    adapter_up_weight,
    row_adapter_index,
    adapter_storage_slot,
):
    n = lax.axis_size("page")
    rows, depth = tokens.shape
    width = adapter_down_weight.shape[1]
    share = adapter_up_weight.shape[1]
    blocks = base_value_weight.shape[1] // share
    adapters = adapter_storage_slot.shape[0]
    cap = rows // 2
    f32, bf16 = jnp.float32, jnp.bfloat16
    return pl.pallas_call(
        functools.partial(gather_kernel, n, adapters),
        out_shape=jax.ShapeDtypeStruct((rows, share), bf16),
        in_specs=[pl.BlockSpec(memory_space=pltpu.HBM)] * 6,
        out_specs=pl.BlockSpec(memory_space=pltpu.VMEM),
        scratch_shapes=[
            pltpu.VMEM((1, rows), jnp.int32),
            pltpu.SMEM((adapters,), jnp.int32),
            pltpu.VMEM((rows, depth), bf16),
            pltpu.VMEM(base_value_weight.shape, bf16),
            pltpu.VMEM((n, depth, width), bf16),
            pltpu.VMEM((n, width, share), bf16),
            pltpu.VMEM((cap, depth), bf16),
            pltpu.VMEM((8, cap), f32),
            pltpu.VMEM((cap, rows), bf16),
            pltpu.VMEM((cap // 2, 128), bf16),
            pltpu.VMEM((cap // 2, 128), bf16),
            pltpu.VMEM((blocks, rows, share), f32),
            pltpu.VMEM((rows, 128), f32),
            pltpu.VMEM((2, rows, share), f32),
            pltpu.VMEM((rows, share), f32),
            pltpu.VMEM((rows // 2, 128), f32),
            pltpu.VMEM((rows // 2, 128), f32),
            pltpu.VMEM((rows // 2, 128), bf16),
            pltpu.VMEM((rows // 2, 128), bf16),
            pltpu.SemaphoreType.DMA((6,)),
            pltpu.SemaphoreType.DMA((n, CHUNKS + 1)),
            pltpu.SemaphoreType.DMA((n, CHUNKS + 1)),
            pltpu.SemaphoreType.DMA((n, CHUNKS + 1)),
            pltpu.SemaphoreType.DMA((3,)),
            pltpu.SemaphoreType.DMA((3,)),
            pltpu.SemaphoreType.DMA((5,)),
            pltpu.SemaphoreType.DMA((5,)),
        ],
        compiler_params=pltpu.CompilerParams(
            collective_id=0, has_side_effects=True, vmem_limit_bytes=60 * 1024 * 1024
        ),
    )(
        tokens,
        base_value_weight,
        adapter_down_weight,
        adapter_up_weight,
        row_adapter_index.reshape(1, rows),
        adapter_storage_slot,
    )


def solution(mesh):
    sizes = mesh.shape
    gathers = sizes["page"] == 4 and sizes["tp"] == 2 and sizes["sub"] == 2
    return jax.shard_map(
        gather_weights_body if gathers else exchange_rows_body,
        mesh=mesh,
        in_specs=(
            P(("grp", "page"), ("tp", "sub")),
            P(("tp", "sub"), None),
            P(("grp", "tp", "sub"), "page"),
            P(("grp", "page"), ("tp", "sub")),
            P(("grp", "page")),
            P("grp"),
        ),
        out_specs=P(("grp", "page"), ("tp", "sub")),
        check_vma=False,
    )
```

```python
import functools

import jax
import jax.numpy as jnp
from jax import lax
from jax.experimental import pallas as pl
from jax.experimental.pallas import tpu as pltpu
from jax.sharding import PartitionSpec as P

ADAPTER_RANK = 64


adapter_scale = 0.5


def rank_within(labels, count):
    onehot = (labels[:, None] == jnp.arange(count, dtype=jnp.int32)[None, :]).astype(jnp.int32)
    before = jnp.cumsum(onehot, axis=0) - onehot
    return jnp.sum(before * onehot, axis=1)


def build_device_worker(down_cols, up_weight_rows):
    width = down_cols.shape[1]
    row_grouping = width // ADAPTER_RANK
    column_group = jnp.arange(width, dtype=jnp.int32) // ADAPTER_RANK

    def owner_work(pair):
        rows, marks = pair
        sources = marks.shape[0]
        count = marks.shape[1]
        feat = rows.shape[2]
        flat_rows = rows.reshape(sources * count, feat)
        owner_ids = marks.reshape(sources * count).astype(jnp.int32)
        select = owner_ids[:, None] == column_group[None, :]
        partial_all = jnp.dot(flat_rows, down_cols, preferred_element_type=jnp.float32)
        picked = (
            jnp.where(select, partial_all, 0.0)
            .reshape(sources * count, row_grouping, ADAPTER_RANK)
            .sum(axis=1)
        )
        shrink_rank = lax.psum(picked, ("tp", "sub")).astype(jnp.bfloat16)
        spread_rows = jnp.where(
            select, jnp.tile(shrink_rank, (1, row_grouping)), jnp.zeros((), jnp.bfloat16)
        )
        expand_rank = (
            jnp.dot(spread_rows, up_weight_rows, preferred_element_type=jnp.float32) * adapter_scale
        )
        return expand_rank.astype(jnp.bfloat16).reshape(sources, count, expand_rank.shape[1])

    return owner_work


def pack_boxes(tokens, flattened, marks, adapter_pages, slot_capacity):
    feat = tokens.shape[1]
    outbox = (
        jnp.zeros((adapter_pages * slot_capacity, feat), jnp.bfloat16).at[flattened].set(tokens)
    )
    labels = (
        jnp.full((adapter_pages * slot_capacity,), -1.0, jnp.bfloat16)
        .at[flattened]
        .set(marks.astype(jnp.bfloat16))
    )
    return (
        outbox.reshape(adapter_pages, slot_capacity, feat),
        labels.reshape(adapter_pages, slot_capacity),
    )


def exchange_rows_body(
    tokens,
    base_value_weight,
    adapter_down_weight,
    adapter_up_weight,
    row_adapter_index,
    adapter_storage_slot,
):
    adapter_pages = lax.axis_size("page")
    row_dev = tokens.shape[0]
    slot_capacity = min(4 * row_dev // adapter_pages, row_dev // 2)
    row_grouping = adapter_down_weight.shape[1] // ADAPTER_RANK
    hits = (
        row_adapter_index[:, None]
        == jnp.arange(adapter_storage_slot.shape[0], dtype=jnp.int32)[None, :]
    )
    storage_position = jnp.sum(jnp.where(hits, adapter_storage_slot[None, :], 0), axis=1)
    target = storage_position // row_grouping
    within = storage_position % row_grouping
    position = rank_within(target, adapter_pages)
    flattened = target * slot_capacity + position
    outbox, labels = pack_boxes(tokens, flattened, within, adapter_pages, slot_capacity)
    device_worker = build_device_worker(adapter_down_weight, adapter_up_weight)
    finished = device_worker(
        (
            lax.all_to_all(outbox, "page", split_axis=0, concat_axis=0, tiled=True),
            lax.all_to_all(labels, "page", split_axis=0, concat_axis=0, tiled=True),
        )
    )
    returned_output = lax.all_to_all(finished, "page", split_axis=0, concat_axis=0, tiled=True)
    adapter_row_output = returned_output.reshape(
        adapter_pages * slot_capacity, returned_output.shape[2]
    )[flattened]
    partial_base = jnp.dot(tokens, base_value_weight, preferred_element_type=jnp.float32)
    base_output_share = lax.psum_scatter(
        partial_base, ("tp", "sub"), scatter_dimension=1, tiled=True
    )
    return (base_output_share + adapter_row_output.astype(jnp.float32)).astype(jnp.bfloat16)


MESH_ID = pl.DeviceIdType.MESH
CHUNKS = 4


def page_in_turn(z, turn, n):
    if turn == 0:
        return z
    nearer = jnp.minimum(z, n - 1 - z)
    step = -((turn + 1) // 2) if turn % 2 else turn // 2
    beyond = jnp.where(z < n - 1 - z, z + (turn - nearer), z - (turn - nearer))
    return jnp.where(turn <= 2 * nearer, z + step, beyond)


def gather_kernel(
    n,
    adapters,
    tokens_hbm,
    base_hbm,
    down_hbm,
    up_hbm,
    index_hbm,
    slot_hbm,
    out_ref,
    index_ref,
    slot_ref,
    tok,
    basew,
    down_all,
    up_all,
    pack,
    pack_slot,
    place,
    pack_send,
    pack_back,
    part,
    picked,
    near_base,
    far_base,
    shrink_send,
    near_shrink,
    far_send,
    far_shrink,
    load_sem,
    right_sem,
    left_sem,
    recv_sem,
    pack_send_sem,
    pack_recv_sem,
    sum_send_sem,
    sum_recv_sem,
):
    z, t, s = lax.axis_index("page"), lax.axis_index("tp"), lax.axis_index("sub")
    rows, depth = tok.shape
    rank = ADAPTER_RANK
    group = down_all.shape[2] // rank
    piece = depth // CHUNKS

    loads = [
        pltpu.make_async_copy(down_hbm, down_all.at[z], load_sem.at[0]),
        pltpu.make_async_copy(up_hbm, up_all.at[z], load_sem.at[1]),
        pltpu.make_async_copy(tokens_hbm, tok, load_sem.at[2]),
        pltpu.make_async_copy(base_hbm, basew, load_sem.at[3]),
        pltpu.make_async_copy(index_hbm, index_ref, load_sem.at[4]),
        pltpu.make_async_copy(slot_hbm, slot_ref, load_sem.at[5]),
    ]
    for load in loads:
        load.start()

    barrier = pltpu.get_barrier_semaphore()
    pl.semaphore_signal(barrier, inc=1, device_id={"tp": 1 - t}, device_id_type=MESH_ID)
    pl.semaphore_signal(barrier, inc=1, device_id={"sub": 1 - s}, device_id_type=MESH_ID)

    @pl.when(z > 0)
    def _():
        pl.semaphore_signal(barrier, inc=1, device_id={"page": z - 1}, device_id_type=MESH_ID)

    @pl.when(z < n - 1)
    def _():
        pl.semaphore_signal(barrier, inc=1, device_id={"page": z + 1}, device_id_type=MESH_ID)

    pl.semaphore_wait(barrier, 2 + (z > 0).astype(jnp.int32) + (z < n - 1).astype(jnp.int32))

    end = (z == 0) | (z == n - 1)
    helped = jnp.where(z == 1, 0, n - 1)
    helper = jnp.where(z == 0, 1, n - 2)
    opposite = n - 1 - z

    def hop(page, chunk, to, sems, own=False):
        if chunk < CHUNKS:
            ref = down_all.at[page, pl.ds(chunk * piece, piece), :]
            src = down_hbm.at[pl.ds(chunk * piece, piece), :] if own else ref
        else:
            ref = up_all.at[page]
            src = up_hbm if own else ref
        return pltpu.make_async_remote_copy(
            src_ref=src,
            dst_ref=ref,
            send_sem=sems.at[page, chunk],
            recv_sem=recv_sem.at[page, chunk],
            device_id={"page": to},
            device_id_type=MESH_ID,
        )

    def goes_right(page, chunk):
        goes = (page <= z) & (z < n - 1)
        return goes & ~((z == n - 2) & (page == 0)) if chunk < CHUNKS else goes

    def goes_left(page, chunk):
        goes = (page >= z) & (z > 0)
        return goes & ~((z == 1) & (page == n - 1)) if chunk < CHUNKS else goes

    def send_on(page, chunk, own=False):
        @pl.when(goes_right(page, chunk))
        def _():
            hop(page, chunk, z + 1, right_sem, own).start()

        @pl.when(goes_left(page, chunk))
        def _():
            hop(page, chunk, z - 1, left_sem, own).start()

    for chunk in (CHUNKS, *range(CHUNKS)):
        send_on(z, chunk, own=True)

    def pack_copy(k, to):
        ref = (pack, pack_slot)[k]
        return pltpu.make_async_remote_copy(
            src_ref=ref,
            dst_ref=ref,
            send_sem=pack_send_sem.at[k],
            recv_sem=pack_recv_sem.at[k],
            device_id={"page": to},
            device_id_type=MESH_ID,
        )

    def pack_return(to):
        return pltpu.make_async_remote_copy(
            src_ref=pack_send,
            dst_ref=pack_back,
            send_sem=pack_send_sem.at[2],
            recv_sem=pack_recv_sem.at[2],
            device_id={"page": to},
            device_id_type=MESH_ID,
        )

    loads[4].wait()
    loads[5].wait()
    slot_row = jnp.zeros(index_ref.shape, jnp.float32)
    for a in range(adapters):
        slot_row = jnp.where(index_ref[...] == a, slot_ref[a].astype(jnp.float32), slot_row)
    slot = jnp.transpose(jnp.broadcast_to(slot_row, (128, rows)))
    lane = lax.broadcasted_iota(jnp.int32, (rows, 128), 1)
    half = (lane // rank).astype(jnp.float32)
    loads[2].wait()
    cap = pack.shape[0]

    @pl.when(end)
    def _():
        lowest = (opposite * group).astype(jnp.float32)
        mine = (slot_row >= lowest) & (slot_row < lowest + float(group))
        marks = jnp.broadcast_to(jnp.where(mine, 1.0, 0.0), (16, rows)).astype(jnp.bfloat16)
        earlier = lax.broadcasted_iota(jnp.int32, (rows, rows), 0) < lax.broadcasted_iota(
            jnp.int32, (rows, rows), 1
        )
        position = jnp.dot(
            marks,
            jnp.where(earlier, 1.0, 0.0).astype(jnp.bfloat16),
            preferred_element_type=jnp.float32,
        )[:1]
        target = jnp.where(mine, position, -1.0)
        spots = lax.broadcasted_iota(jnp.int32, (cap, rows), 0).astype(jnp.float32)
        place[...] = jnp.where(spots == target, 1.0, 0.0).astype(jnp.bfloat16)

        @pl.loop(0, depth // 512)
        def _(b):
            columns = pl.ds(pl.multiple_of(b * 512, 512), 512)
            pack[:, columns] = jnp.dot(
                place[...], tok[:, columns], preferred_element_type=jnp.float32
            ).astype(jnp.bfloat16)

        pack_slot[...] = lax.dot_general(
            jnp.broadcast_to(slot_row, (16, rows)).astype(jnp.bfloat16),
            place[...],
            (((1,), (1,)), ((), ())),
            preferred_element_type=jnp.float32,
        )[: pack_slot.shape[0]]
        for k in range(2):
            pack_copy(k, helper).start()

    loads[3].wait()
    blocks, width = part.shape[0], part.shape[2]

    @pl.loop(0, blocks)
    def _(b):
        columns = pl.ds(pl.multiple_of(b * width, width), width)
        part[b] = jnp.dot(tok[...], basew[:, columns], preferred_element_type=jnp.float32)

    def to_sibling(k):
        return pltpu.make_async_remote_copy(
            src_ref=part.at[2 * k + 1 - s],
            dst_ref=near_base.at[k],
            send_sem=sum_send_sem.at[k],
            recv_sem=sum_recv_sem.at[k],
            device_id={"sub": 1 - s},
            device_id_type=MESH_ID,
        )

    base_far = pltpu.make_async_remote_copy(
        src_ref=part.at[2 * (1 - t) + s],
        dst_ref=far_base,
        send_sem=sum_send_sem.at[2],
        recv_sem=sum_recv_sem.at[2],
        device_id={"tp": 1 - t},
        device_id_type=MESH_ID,
    )
    for k in range(2):
        to_sibling(k).start()

    def pick(page, product, slot, half):
        first = (page * group).astype(jnp.float32) + half
        total = jnp.zeros(slot.shape, jnp.float32)
        for g in range(group * rank // 128):
            hit = slot == first + float(g * (128 // rank))
            total += jnp.where(hit, product[:, g * 128 : g * 128 + 128], 0.0)
        return total

    def product_of(ref, page, chunk):
        return jnp.dot(
            ref[:, chunk * piece : chunk * piece + piece],
            down_all[page, pl.ds(chunk * piece, piece), :],
            preferred_element_type=jnp.float32,
        )

    def take_piece(page, chunk):
        picked[...] += pick(page, product_of(tok, page, chunk), slot, half)

    def pass_on(page, chunk):
        hop(page, chunk, z, left_sem).wait_recv()
        send_on(page, chunk)

    loads[0].wait()
    loads[1].wait()
    picked[...] = jnp.zeros_like(picked)
    for chunk in range(CHUNKS):
        take_piece(z, chunk)
    for k in range(2):
        to_sibling(k).wait_recv()
    part[2 * (1 - t) + s] += near_base[1 - t]
    base_far.start()
    last = page_in_turn(z, n - 1, n)
    between = [page_in_turn(z, turn, n) for turn in range(1, n - 1)]
    for page in between:
        pass_on(page, CHUNKS)

    @pl.when(~end)
    def _():
        for chunk in range(CHUNKS):
            for page in between:
                pass_on(page, chunk)
            for page in between:
                take_piece(page, chunk)

    @pl.when(end)
    def _():
        for page in between:
            for chunk in range(CHUNKS):
                pass_on(page, chunk)
                take_piece(page, chunk)

    pass_on(last, CHUNKS)

    @pl.when(~end)
    def _():
        for k in range(2):
            pack_copy(k, z).wait_recv()
        their_slot = jnp.transpose(jnp.broadcast_to(pack_slot[:1], (128, cap)))
        theirs = jnp.zeros((cap, 128), jnp.float32)
        for chunk in range(CHUNKS):
            pass_on(last, chunk)
            theirs += pick(last, product_of(pack, last, chunk), their_slot, half[:cap])
            if chunk < CHUNKS - 1:
                take_piece(last, chunk)
        theirs += pltpu.roll(theirs, rank, 1)
        pack_send[...] = jnp.where(
            lane[: cap // 2] < rank, theirs[: cap // 2], theirs[cap // 2 :]
        ).astype(jnp.bfloat16)
        pack_return(helped).start()
        take_piece(last, CHUNKS - 1)

    @pl.when(end)
    def _():
        pack_return(z).wait_recv()
        back = pack_back[...].astype(jnp.float32)
        back = jnp.concatenate([back, pltpu.roll(back, rank, 1)], axis=0)
        back = jnp.where(lane[:cap] < rank, back, 0.0).astype(jnp.bfloat16)
        picked[...] += lax.dot_general(
            place[...], back, (((0,), (0,)), ((), ())), preferred_element_type=jnp.float32
        )

    folded = picked[...] + pltpu.roll(picked[...], rank, 1)
    low = lane[: rows // 2] < rank
    shrink_send[...] = jnp.where(low, folded[: rows // 2], folded[rows // 2 :])
    near = pltpu.make_async_remote_copy(
        src_ref=shrink_send,
        dst_ref=near_shrink,
        send_sem=sum_send_sem.at[3],
        recv_sem=sum_recv_sem.at[3],
        device_id={"sub": 1 - s},
        device_id_type=MESH_ID,
    )
    near.start()
    near.wait_recv()
    chip_sum = shrink_send[...] + near_shrink[...]
    far_send[...] = chip_sum.astype(jnp.bfloat16)
    far = pltpu.make_async_remote_copy(
        src_ref=far_send,
        dst_ref=far_shrink,
        send_sem=sum_send_sem.at[4],
        recv_sem=sum_recv_sem.at[4],
        device_id={"tp": 1 - t},
        device_id_type=MESH_ID,
    )
    far.start()
    base_far.wait_recv()
    part[2 * t + s] += near_base[t] + far_base[...]
    far.wait_recv()
    both = chip_sum + far_shrink[...].astype(jnp.float32)
    both = both.astype(jnp.bfloat16).astype(jnp.float32)
    turned = pltpu.roll(both, rank, 1)
    shrink = jnp.concatenate(
        [jnp.where(low, both, turned), jnp.where(low, turned, both)], axis=0
    )
    spread = jnp.concatenate(
        [
            jnp.where(slot == half + float(b * (128 // rank)), shrink, 0.0).astype(jnp.bfloat16)
            for b in range(n * group * rank // 128)
        ],
        axis=1,
    )
    expand = jnp.dot(
        spread,
        up_all[...].reshape(n * group * rank, up_all.shape[2]),
        preferred_element_type=jnp.float32,
    )
    lora = (expand * adapter_scale).astype(jnp.bfloat16).astype(jnp.float32)
    out_ref[...] = (part[2 * t + s] + lora).astype(jnp.bfloat16)

    for k in range(2):
        to_sibling(k).wait_send()
    base_far.wait_send()
    near.wait_send()
    far.wait_send()

    @pl.when(end)
    def _():
        for k in range(2):
            pack_copy(k, helper).wait_send()

    @pl.when(~end)
    def _():
        pack_return(helped).wait_send()

    for turn in range(n):
        page = page_in_turn(z, turn, n)
        for chunk in range(CHUNKS + 1):

            @pl.when(goes_right(page, chunk))
            def _():
                hop(page, chunk, z + 1, right_sem, turn == 0).wait_send()

            @pl.when(goes_left(page, chunk))
            def _():
                hop(page, chunk, z - 1, left_sem, turn == 0).wait_send()


def gather_weights_body(
    tokens,
    base_value_weight,
    adapter_down_weight,
    adapter_up_weight,
    row_adapter_index,
    adapter_storage_slot,
):
    n = lax.axis_size("page")
    rows, depth = tokens.shape
    width = adapter_down_weight.shape[1]
    share = adapter_up_weight.shape[1]
    blocks = base_value_weight.shape[1] // share
    adapters = adapter_storage_slot.shape[0]
    cap = rows // 2
    f32, bf16 = jnp.float32, jnp.bfloat16
    return pl.pallas_call(
        functools.partial(gather_kernel, n, adapters),
        out_shape=jax.ShapeDtypeStruct((rows, share), bf16),
        in_specs=[pl.BlockSpec(memory_space=pltpu.HBM)] * 6,
        out_specs=pl.BlockSpec(memory_space=pltpu.VMEM),
        scratch_shapes=[
            pltpu.VMEM((1, rows), jnp.int32),
            pltpu.SMEM((adapters,), jnp.int32),
            pltpu.VMEM((rows, depth), bf16),
            pltpu.VMEM(base_value_weight.shape, bf16),
            pltpu.VMEM((n, depth, width), bf16),
            pltpu.VMEM((n, width, share), bf16),
            pltpu.VMEM((cap, depth), bf16),
            pltpu.VMEM((8, cap), f32),
            pltpu.VMEM((cap, rows), bf16),
            pltpu.VMEM((cap // 2, 128), bf16),
            pltpu.VMEM((cap // 2, 128), bf16),
            pltpu.VMEM((blocks, rows, share), f32),
            pltpu.VMEM((rows, 128), f32),
            pltpu.VMEM((2, rows, share), f32),
            pltpu.VMEM((rows, share), f32),
            pltpu.VMEM((rows // 2, 128), f32),
            pltpu.VMEM((rows // 2, 128), f32),
            pltpu.VMEM((rows // 2, 128), bf16),
            pltpu.VMEM((rows // 2, 128), bf16),
            pltpu.SemaphoreType.DMA((6,)),
            pltpu.SemaphoreType.DMA((n, CHUNKS + 1)),
            pltpu.SemaphoreType.DMA((n, CHUNKS + 1)),
            pltpu.SemaphoreType.DMA((n, CHUNKS + 1)),
            pltpu.SemaphoreType.DMA((3,)),
            pltpu.SemaphoreType.DMA((3,)),
            pltpu.SemaphoreType.DMA((5,)),
            pltpu.SemaphoreType.DMA((5,)),
        ],
        compiler_params=pltpu.CompilerParams(
            collective_id=0, has_side_effects=True, vmem_limit_bytes=60 * 1024 * 1024
        ),
    )(
        tokens,
        base_value_weight,
        adapter_down_weight,
        adapter_up_weight,
        row_adapter_index.reshape(1, rows),
        adapter_storage_slot,
    )


def solution(mesh):
    sizes = mesh.shape
    gathers = sizes["page"] == 4 and sizes["tp"] == 2 and sizes["sub"] == 2
    return jax.shard_map(
        gather_weights_body if gathers else exchange_rows_body,
        mesh=mesh,
        in_specs=(
            P(("grp", "page"), ("tp", "sub")),
            P(("tp", "sub"), None),
            P(("grp", "tp", "sub"), "page"),
            P(("grp", "page"), ("tp", "sub")),
            P(("grp", "page")),
            P("grp"),
        ),
        out_specs=P(("grp", "page"), ("tp", "sub")),
        check_vma=False,
    )
```

```python
import functools

import jax
import jax.numpy as jnp
from jax import lax
from jax.experimental import pallas as pl
from jax.experimental.pallas import tpu as pltpu
from jax.sharding import PartitionSpec as P

ADAPTER_RANK = 64


adapter_scale = 0.5


def rank_within(labels, count):
    onehot = (labels[:, None] == jnp.arange(count, dtype=jnp.int32)[None, :]).astype(jnp.int32)
    before = jnp.cumsum(onehot, axis=0) - onehot
    return jnp.sum(before * onehot, axis=1)


def build_device_worker(down_cols, up_weight_rows):
    width = down_cols.shape[1]
    row_grouping = width // ADAPTER_RANK
    column_group = jnp.arange(width, dtype=jnp.int32) // ADAPTER_RANK

    def owner_work(pair):
        rows, marks = pair
        sources = marks.shape[0]
        count = marks.shape[1]
        feat = rows.shape[2]
        flat_rows = rows.reshape(sources * count, feat)
        owner_ids = marks.reshape(sources * count).astype(jnp.int32)
        select = owner_ids[:, None] == column_group[None, :]
        partial_all = jnp.dot(flat_rows, down_cols, preferred_element_type=jnp.float32)
        picked = (
            jnp.where(select, partial_all, 0.0)
            .reshape(sources * count, row_grouping, ADAPTER_RANK)
            .sum(axis=1)
        )
        shrink_rank = lax.psum(picked, ("tp", "sub")).astype(jnp.bfloat16)
        spread_rows = jnp.where(
            select, jnp.tile(shrink_rank, (1, row_grouping)), jnp.zeros((), jnp.bfloat16)
        )
        expand_rank = (
            jnp.dot(spread_rows, up_weight_rows, preferred_element_type=jnp.float32) * adapter_scale
        )
        return expand_rank.astype(jnp.bfloat16).reshape(sources, count, expand_rank.shape[1])

    return owner_work


def pack_boxes(tokens, flattened, marks, adapter_pages, slot_capacity):
    feat = tokens.shape[1]
    outbox = (
        jnp.zeros((adapter_pages * slot_capacity, feat), jnp.bfloat16).at[flattened].set(tokens)
    )
    labels = (
        jnp.full((adapter_pages * slot_capacity,), -1.0, jnp.bfloat16)
        .at[flattened]
        .set(marks.astype(jnp.bfloat16))
    )
    return (
        outbox.reshape(adapter_pages, slot_capacity, feat),
        labels.reshape(adapter_pages, slot_capacity),
    )


def exchange_rows_body(
    tokens,
    base_value_weight,
    adapter_down_weight,
    adapter_up_weight,
    row_adapter_index,
    adapter_storage_slot,
):
    adapter_pages = lax.axis_size("page")
    row_dev = tokens.shape[0]
    slot_capacity = min(4 * row_dev // adapter_pages, row_dev // 2)
    row_grouping = adapter_down_weight.shape[1] // ADAPTER_RANK
    hits = (
        row_adapter_index[:, None]
        == jnp.arange(adapter_storage_slot.shape[0], dtype=jnp.int32)[None, :]
    )
    storage_position = jnp.sum(jnp.where(hits, adapter_storage_slot[None, :], 0), axis=1)
    target = storage_position // row_grouping
    within = storage_position % row_grouping
    position = rank_within(target, adapter_pages)
    flattened = target * slot_capacity + position
    outbox, labels = pack_boxes(tokens, flattened, within, adapter_pages, slot_capacity)
    device_worker = build_device_worker(adapter_down_weight, adapter_up_weight)
    finished = device_worker(
        (
            lax.all_to_all(outbox, "page", split_axis=0, concat_axis=0, tiled=True),
            lax.all_to_all(labels, "page", split_axis=0, concat_axis=0, tiled=True),
        )
    )
    returned_output = lax.all_to_all(finished, "page", split_axis=0, concat_axis=0, tiled=True)
    adapter_row_output = returned_output.reshape(
        adapter_pages * slot_capacity, returned_output.shape[2]
    )[flattened]
    partial_base = jnp.dot(tokens, base_value_weight, preferred_element_type=jnp.float32)
    base_output_share = lax.psum_scatter(
        partial_base, ("tp", "sub"), scatter_dimension=1, tiled=True
    )
    return (base_output_share + adapter_row_output.astype(jnp.float32)).astype(jnp.bfloat16)


MESH_ID = pl.DeviceIdType.MESH
BOUNDS = (0, 2, 8, 12, 16)
CHUNKS = len(BOUNDS) - 1


def piece_of(chunk, depth):
    return BOUNDS[chunk] * depth // 16, (BOUNDS[chunk + 1] - BOUNDS[chunk]) * depth // 16


def page_in_turn(z, turn, n):
    if turn == 0:
        return z
    nearer = jnp.minimum(z, n - 1 - z)
    step = -((turn + 1) // 2) if turn % 2 else turn // 2
    beyond = jnp.where(z < n - 1 - z, z + (turn - nearer), z - (turn - nearer))
    return jnp.where(turn <= 2 * nearer, z + step, beyond)


def gather_kernel(
    n,
    adapters,
    tokens_hbm,
    base_hbm,
    down_hbm,
    up_hbm,
    index_hbm,
    slot_hbm,
    out_ref,
    index_ref,
    slot_ref,
    tok,
    basew,
    down_all,
    up_all,
    pack,
    pack_first,
    pack_slot,
    place,
    pack_send,
    pack_back,
    part,
    picked,
    near_base,
    far_base,
    shrink_send,
    near_shrink,
    far_send,
    far_shrink,
    load_sem,
    right_sem,
    left_sem,
    recv_sem,
    pack_send_sem,
    pack_recv_sem,
    sum_send_sem,
    sum_recv_sem,
):
    z, t, s = lax.axis_index("page"), lax.axis_index("tp"), lax.axis_index("sub")
    rows, depth = tok.shape
    rank = ADAPTER_RANK
    group = down_all.shape[2] // rank

    loads = [
        pltpu.make_async_copy(down_hbm, down_all.at[z], load_sem.at[0]),
        pltpu.make_async_copy(up_hbm, up_all.at[z], load_sem.at[1]),
        pltpu.make_async_copy(tokens_hbm, tok, load_sem.at[2]),
        pltpu.make_async_copy(base_hbm, basew, load_sem.at[3]),
        pltpu.make_async_copy(index_hbm, index_ref, load_sem.at[4]),
        pltpu.make_async_copy(slot_hbm, slot_ref, load_sem.at[5]),
    ]
    for load in loads:
        load.start()

    barrier = pltpu.get_barrier_semaphore()
    pl.semaphore_signal(barrier, inc=1, device_id={"tp": 1 - t}, device_id_type=MESH_ID)
    pl.semaphore_signal(barrier, inc=1, device_id={"sub": 1 - s}, device_id_type=MESH_ID)

    @pl.when(z > 0)
    def _():
        pl.semaphore_signal(barrier, inc=1, device_id={"page": z - 1}, device_id_type=MESH_ID)

    @pl.when(z < n - 1)
    def _():
        pl.semaphore_signal(barrier, inc=1, device_id={"page": z + 1}, device_id_type=MESH_ID)

    pl.semaphore_wait(barrier, 2 + (z > 0).astype(jnp.int32) + (z < n - 1).astype(jnp.int32))

    end = (z == 0) | (z == n - 1)
    helped = jnp.where(z == 1, 0, n - 1)
    helper = jnp.where(z == 0, 1, n - 2)
    opposite = n - 1 - z
    second = jnp.where(z == 0, n - 2, 1)

    def hop(page, chunk, to, sems, own=False):
        if chunk < CHUNKS:
            span = pl.ds(*piece_of(chunk, depth))
            ref = down_all.at[page, span, :]
            src = down_hbm.at[span, :] if own else ref
        else:
            ref = up_all.at[page]
            src = up_hbm if own else ref
        return pltpu.make_async_remote_copy(
            src_ref=src,
            dst_ref=ref,
            send_sem=sems.at[page, chunk],
            recv_sem=recv_sem.at[page, chunk],
            device_id={"page": to},
            device_id_type=MESH_ID,
        )

    def goes_right(page, chunk):
        goes = (page <= z) & (z < n - 1)
        if chunk == 0:
            return goes & ~((z == n - 2) & (page <= 1))
        return goes & ~((z == n - 2) & (page == 0)) if chunk < CHUNKS else goes

    def goes_left(page, chunk):
        goes = (page >= z) & (z > 0)
        if chunk == 0:
            return goes & ~((z == 1) & (page >= n - 2))
        return goes & ~((z == 1) & (page == n - 1)) if chunk < CHUNKS else goes

    def send_on(page, chunk, own=False):
        @pl.when(goes_right(page, chunk))
        def _():
            hop(page, chunk, z + 1, right_sem, own).start()

        @pl.when(goes_left(page, chunk))
        def _():
            hop(page, chunk, z - 1, left_sem, own).start()

    for chunk in (CHUNKS, *range(CHUNKS)):
        send_on(z, chunk, own=True)

    def pack_copy(k, to):
        ref = (pack, pack_slot.at[0], pack_first, pack_slot.at[1])[k]
        return pltpu.make_async_remote_copy(
            src_ref=ref,
            dst_ref=ref,
            send_sem=pack_send_sem.at[k],
            recv_sem=pack_recv_sem.at[k],
            device_id={"page": to},
            device_id_type=MESH_ID,
        )

    def pack_return(k, to):
        return pltpu.make_async_remote_copy(
            src_ref=pack_send.at[k],
            dst_ref=pack_back.at[k],
            send_sem=pack_send_sem.at[4 + k],
            recv_sem=pack_recv_sem.at[4 + k],
            device_id={"page": to},
            device_id_type=MESH_ID,
        )

    loads[4].wait()
    loads[5].wait()
    slot_row = jnp.zeros(index_ref.shape, jnp.float32)
    for a in range(adapters):
        slot_row = jnp.where(index_ref[...] == a, slot_ref[a].astype(jnp.float32), slot_row)
    slot = jnp.transpose(jnp.broadcast_to(slot_row, (128, rows)))
    lane = lax.broadcasted_iota(jnp.int32, (rows, 128), 1)
    half = (lane // rank).astype(jnp.float32)
    loads[2].wait()
    cap = pack.shape[0]

    @pl.when(end)
    def _():
        earlier = lax.broadcasted_iota(jnp.int32, (rows, rows), 0) < lax.broadcasted_iota(
            jnp.int32, (rows, rows), 1
        )
        earlier = jnp.where(earlier, 1.0, 0.0).astype(jnp.bfloat16)
        spots = lax.broadcasted_iota(jnp.int32, (cap, rows), 0).astype(jnp.float32)
        for k, page in ((1, second), (0, opposite)):
            lowest = (page * group).astype(jnp.float32)
            mine = (slot_row >= lowest) & (slot_row < lowest + float(group))
            marks = jnp.broadcast_to(jnp.where(mine, 1.0, 0.0), (16, rows)).astype(jnp.bfloat16)
            position = jnp.dot(marks, earlier, preferred_element_type=jnp.float32)[:1]
            target = jnp.where(mine, position, -1.0)
            place[k] = jnp.where(spots == target, 1.0, 0.0).astype(jnp.bfloat16)
            if k:
                pack_first[...] = jnp.dot(
                    place[k],
                    tok[:, pl.ds(*piece_of(0, depth))],
                    preferred_element_type=jnp.float32,
                ).astype(jnp.bfloat16)
            else:

                @pl.loop(0, depth // 512)
                def _(b):
                    columns = pl.ds(pl.multiple_of(b * 512, 512), 512)
                    pack[:, columns] = jnp.dot(
                        place[0], tok[:, columns], preferred_element_type=jnp.float32
                    ).astype(jnp.bfloat16)

            pack_slot[k] = lax.dot_general(
                jnp.broadcast_to(slot_row, (16, rows)).astype(jnp.bfloat16),
                place[k],
                (((1,), (1,)), ((), ())),
                preferred_element_type=jnp.float32,
            )[: pack_slot.shape[1]]
            for c in range(2 * k, 2 * k + 2):
                pack_copy(c, helper).start()

    loads[3].wait()
    blocks, width = part.shape[0], part.shape[2]

    @pl.loop(0, blocks)
    def _(b):
        columns = pl.ds(pl.multiple_of(b * width, width), width)
        part[b] = jnp.dot(tok[...], basew[:, columns], preferred_element_type=jnp.float32)

    def to_sibling(k):
        return pltpu.make_async_remote_copy(
            src_ref=part.at[2 * k + 1 - s],
            dst_ref=near_base.at[k],
            send_sem=sum_send_sem.at[k],
            recv_sem=sum_recv_sem.at[k],
            device_id={"sub": 1 - s},
            device_id_type=MESH_ID,
        )

    base_far = pltpu.make_async_remote_copy(
        src_ref=part.at[2 * (1 - t) + s],
        dst_ref=far_base,
        send_sem=sum_send_sem.at[2],
        recv_sem=sum_recv_sem.at[2],
        device_id={"tp": 1 - t},
        device_id_type=MESH_ID,
    )
    for k in range(2):
        to_sibling(k).start()

    def pick(page, product, slot, half):
        first = (page * group).astype(jnp.float32) + half
        total = jnp.zeros(slot.shape, jnp.float32)
        for g in range(group * rank // 128):
            hit = slot == first + float(g * (128 // rank))
            total += jnp.where(hit, product[:, g * 128 : g * 128 + 128], 0.0)
        return total

    def product_of(ref, page, chunk):
        return jnp.dot(
            ref[:, pl.ds(*piece_of(chunk, depth))],
            down_all[page, pl.ds(*piece_of(chunk, depth)), :],
            preferred_element_type=jnp.float32,
        )

    def take_piece(page, chunk):
        picked[...] += pick(page, product_of(tok, page, chunk), slot, half)

    def pass_on(page, chunk):
        hop(page, chunk, z, left_sem).wait_recv()
        send_on(page, chunk)

    loads[0].wait()
    loads[1].wait()
    picked[...] = jnp.zeros_like(picked)
    for chunk in range(CHUNKS):
        take_piece(z, chunk)
    for k in range(2):
        to_sibling(k).wait_recv()
    part[2 * (1 - t) + s] += near_base[1 - t]
    base_far.start()
    last = page_in_turn(z, n - 1, n)
    between = [page_in_turn(z, turn, n) for turn in range(1, n - 1)]
    for page in between:
        pass_on(page, CHUNKS)

    def return_pack(k, theirs):
        theirs += pltpu.roll(theirs, rank, 1)
        pack_send[k] = jnp.where(
            lane[: cap // 2] < rank, theirs[: cap // 2], theirs[cap // 2 :]
        ).astype(jnp.bfloat16)
        pack_return(k, helped).start()

    def slot_of_pack(k):
        pack_copy(2 * k, z).wait_recv()
        pack_copy(2 * k + 1, z).wait_recv()
        return jnp.transpose(jnp.broadcast_to(pack_slot[k, :1], (128, cap)))

    def place_back(k):
        pack_return(k, z).wait_recv()
        back = pack_back[k].astype(jnp.float32)
        back = jnp.concatenate([back, pltpu.roll(back, rank, 1)], axis=0)
        back = jnp.where(lane[:cap] < rank, back, 0.0).astype(jnp.bfloat16)
        picked[...] += lax.dot_general(
            place[k], back, (((0,), (0,)), ((), ())), preferred_element_type=jnp.float32
        )

    @pl.when(~end)
    def _():
        for chunk in range(CHUNKS):
            for page in between:
                pass_on(page, chunk)
            for page in between:
                take_piece(page, chunk)
        pass_on(last, CHUNKS)
        first_slot = slot_of_pack(1)
        product = jnp.dot(
            pack_first[...],
            down_all[opposite, pl.ds(*piece_of(0, depth)), :],
            preferred_element_type=jnp.float32,
        )
        return_pack(1, pick(opposite, product, first_slot, half[:cap]))
        their_slot = slot_of_pack(0)
        theirs = jnp.zeros((cap, 128), jnp.float32)
        for chunk in range(CHUNKS):
            pass_on(last, chunk)
            theirs += pick(last, product_of(pack, last, chunk), their_slot, half[:cap])
            if chunk < CHUNKS - 1:
                take_piece(last, chunk)
        return_pack(0, theirs)
        take_piece(last, CHUNKS - 1)

    @pl.when(end)
    def _():
        for turn, page in enumerate(between):
            for chunk in range(turn, CHUNKS):
                pass_on(page, chunk)
                take_piece(page, chunk)
        place_back(1)
        pass_on(last, CHUNKS)
        place_back(0)

    folded = picked[...] + pltpu.roll(picked[...], rank, 1)
    low = lane[: rows // 2] < rank
    shrink_send[...] = jnp.where(low, folded[: rows // 2], folded[rows // 2 :])
    near = pltpu.make_async_remote_copy(
        src_ref=shrink_send,
        dst_ref=near_shrink,
        send_sem=sum_send_sem.at[3],
        recv_sem=sum_recv_sem.at[3],
        device_id={"sub": 1 - s},
        device_id_type=MESH_ID,
    )
    near.start()
    near.wait_recv()
    chip_sum = shrink_send[...] + near_shrink[...]
    far_send[...] = chip_sum.astype(jnp.bfloat16)
    far = pltpu.make_async_remote_copy(
        src_ref=far_send,
        dst_ref=far_shrink,
        send_sem=sum_send_sem.at[4],
        recv_sem=sum_recv_sem.at[4],
        device_id={"tp": 1 - t},
        device_id_type=MESH_ID,
    )
    far.start()
    base_far.wait_recv()
    part[2 * t + s] += near_base[t] + far_base[...]
    far.wait_recv()
    both = chip_sum + far_shrink[...].astype(jnp.float32)
    both = both.astype(jnp.bfloat16).astype(jnp.float32)
    turned = pltpu.roll(both, rank, 1)
    shrink = jnp.concatenate(
        [jnp.where(low, both, turned), jnp.where(low, turned, both)], axis=0
    )
    spread = jnp.concatenate(
        [
            jnp.where(slot == half + float(b * (128 // rank)), shrink, 0.0).astype(jnp.bfloat16)
            for b in range(n * group * rank // 128)
        ],
        axis=1,
    )
    expand = jnp.dot(
        spread,
        up_all[...].reshape(n * group * rank, up_all.shape[2]),
        preferred_element_type=jnp.float32,
    )
    lora = (expand * adapter_scale).astype(jnp.bfloat16).astype(jnp.float32)
    out_ref[...] = (part[2 * t + s] + lora).astype(jnp.bfloat16)

    for k in range(2):
        to_sibling(k).wait_send()
    base_far.wait_send()
    near.wait_send()
    far.wait_send()

    @pl.when(end)
    def _():
        for k in range(4):
            pack_copy(k, helper).wait_send()

    @pl.when(~end)
    def _():
        for k in range(2):
            pack_return(k, helped).wait_send()

    for turn in range(n):
        page = page_in_turn(z, turn, n)
        for chunk in range(CHUNKS + 1):

            @pl.when(goes_right(page, chunk))
            def _():
                hop(page, chunk, z + 1, right_sem, turn == 0).wait_send()

            @pl.when(goes_left(page, chunk))
            def _():
                hop(page, chunk, z - 1, left_sem, turn == 0).wait_send()


def gather_weights_body(
    tokens,
    base_value_weight,
    adapter_down_weight,
    adapter_up_weight,
    row_adapter_index,
    adapter_storage_slot,
):
    n = lax.axis_size("page")
    rows, depth = tokens.shape
    width = adapter_down_weight.shape[1]
    share = adapter_up_weight.shape[1]
    blocks = base_value_weight.shape[1] // share
    adapters = adapter_storage_slot.shape[0]
    cap = rows // 2
    f32, bf16 = jnp.float32, jnp.bfloat16
    return pl.pallas_call(
        functools.partial(gather_kernel, n, adapters),
        out_shape=jax.ShapeDtypeStruct((rows, share), bf16),
        in_specs=[pl.BlockSpec(memory_space=pltpu.HBM)] * 6,
        out_specs=pl.BlockSpec(memory_space=pltpu.VMEM),
        scratch_shapes=[
            pltpu.VMEM((1, rows), jnp.int32),
            pltpu.SMEM((adapters,), jnp.int32),
            pltpu.VMEM((rows, depth), bf16),
            pltpu.VMEM(base_value_weight.shape, bf16),
            pltpu.VMEM((n, depth, width), bf16),
            pltpu.VMEM((n, width, share), bf16),
            pltpu.VMEM((cap, depth), bf16),
            pltpu.VMEM((cap, piece_of(0, depth)[1]), bf16),
            pltpu.VMEM((2, 8, cap), f32),
            pltpu.VMEM((2, cap, rows), bf16),
            pltpu.VMEM((2, cap // 2, 128), bf16),
            pltpu.VMEM((2, cap // 2, 128), bf16),
            pltpu.VMEM((blocks, rows, share), f32),
            pltpu.VMEM((rows, 128), f32),
            pltpu.VMEM((2, rows, share), f32),
            pltpu.VMEM((rows, share), f32),
            pltpu.VMEM((rows // 2, 128), f32),
            pltpu.VMEM((rows // 2, 128), f32),
            pltpu.VMEM((rows // 2, 128), bf16),
            pltpu.VMEM((rows // 2, 128), bf16),
            pltpu.SemaphoreType.DMA((6,)),
            pltpu.SemaphoreType.DMA((n, CHUNKS + 1)),
            pltpu.SemaphoreType.DMA((n, CHUNKS + 1)),
            pltpu.SemaphoreType.DMA((n, CHUNKS + 1)),
            pltpu.SemaphoreType.DMA((6,)),
            pltpu.SemaphoreType.DMA((6,)),
            pltpu.SemaphoreType.DMA((5,)),
            pltpu.SemaphoreType.DMA((5,)),
        ],
        compiler_params=pltpu.CompilerParams(
            collective_id=0, has_side_effects=True, vmem_limit_bytes=60 * 1024 * 1024
        ),
    )(
        tokens,
        base_value_weight,
        adapter_down_weight,
        adapter_up_weight,
        row_adapter_index.reshape(1, rows),
        adapter_storage_slot,
    )


def solution(mesh):
    sizes = mesh.shape
    gathers = sizes["page"] == 4 and sizes["tp"] == 2 and sizes["sub"] == 2
    return jax.shard_map(
        gather_weights_body if gathers else exchange_rows_body,
        mesh=mesh,
        in_specs=(
            P(("grp", "page"), ("tp", "sub")),
            P(("tp", "sub"), None),
            P(("grp", "tp", "sub"), "page"),
            P(("grp", "page"), ("tp", "sub")),
            P(("grp", "page")),
            P("grp"),
        ),
        out_specs=P(("grp", "page"), ("tp", "sub")),
        check_vma=False,
    )
```

```python
import functools

import jax
import jax.numpy as jnp
from jax import lax
from jax.experimental import pallas as pl
from jax.experimental.pallas import tpu as pltpu
from jax.sharding import PartitionSpec as P

ADAPTER_RANK = 64


adapter_scale = 0.5


def rank_within(labels, count):
    onehot = (labels[:, None] == jnp.arange(count, dtype=jnp.int32)[None, :]).astype(jnp.int32)
    before = jnp.cumsum(onehot, axis=0) - onehot
    return jnp.sum(before * onehot, axis=1)


def build_device_worker(down_cols, up_weight_rows):
    width = down_cols.shape[1]
    row_grouping = width // ADAPTER_RANK
    column_group = jnp.arange(width, dtype=jnp.int32) // ADAPTER_RANK

    def owner_work(pair):
        rows, marks = pair
        sources = marks.shape[0]
        count = marks.shape[1]
        feat = rows.shape[2]
        flat_rows = rows.reshape(sources * count, feat)
        owner_ids = marks.reshape(sources * count).astype(jnp.int32)
        select = owner_ids[:, None] == column_group[None, :]
        partial_all = jnp.dot(flat_rows, down_cols, preferred_element_type=jnp.float32)
        picked = (
            jnp.where(select, partial_all, 0.0)
            .reshape(sources * count, row_grouping, ADAPTER_RANK)
            .sum(axis=1)
        )
        shrink_rank = lax.psum(picked, ("tp", "sub")).astype(jnp.bfloat16)
        spread_rows = jnp.where(
            select, jnp.tile(shrink_rank, (1, row_grouping)), jnp.zeros((), jnp.bfloat16)
        )
        expand_rank = (
            jnp.dot(spread_rows, up_weight_rows, preferred_element_type=jnp.float32) * adapter_scale
        )
        return expand_rank.astype(jnp.bfloat16).reshape(sources, count, expand_rank.shape[1])

    return owner_work


def pack_boxes(tokens, flattened, marks, adapter_pages, slot_capacity):
    feat = tokens.shape[1]
    outbox = (
        jnp.zeros((adapter_pages * slot_capacity, feat), jnp.bfloat16).at[flattened].set(tokens)
    )
    labels = (
        jnp.full((adapter_pages * slot_capacity,), -1.0, jnp.bfloat16)
        .at[flattened]
        .set(marks.astype(jnp.bfloat16))
    )
    return (
        outbox.reshape(adapter_pages, slot_capacity, feat),
        labels.reshape(adapter_pages, slot_capacity),
    )


def exchange_rows_body(
    tokens,
    base_value_weight,
    adapter_down_weight,
    adapter_up_weight,
    row_adapter_index,
    adapter_storage_slot,
):
    adapter_pages = lax.axis_size("page")
    row_dev = tokens.shape[0]
    slot_capacity = min(4 * row_dev // adapter_pages, row_dev // 2)
    row_grouping = adapter_down_weight.shape[1] // ADAPTER_RANK
    hits = (
        row_adapter_index[:, None]
        == jnp.arange(adapter_storage_slot.shape[0], dtype=jnp.int32)[None, :]
    )
    storage_position = jnp.sum(jnp.where(hits, adapter_storage_slot[None, :], 0), axis=1)
    target = storage_position // row_grouping
    within = storage_position % row_grouping
    position = rank_within(target, adapter_pages)
    flattened = target * slot_capacity + position
    outbox, labels = pack_boxes(tokens, flattened, within, adapter_pages, slot_capacity)
    device_worker = build_device_worker(adapter_down_weight, adapter_up_weight)
    finished = device_worker(
        (
            lax.all_to_all(outbox, "page", split_axis=0, concat_axis=0, tiled=True),
            lax.all_to_all(labels, "page", split_axis=0, concat_axis=0, tiled=True),
        )
    )
    returned_output = lax.all_to_all(finished, "page", split_axis=0, concat_axis=0, tiled=True)
    adapter_row_output = returned_output.reshape(
        adapter_pages * slot_capacity, returned_output.shape[2]
    )[flattened]
    partial_base = jnp.dot(tokens, base_value_weight, preferred_element_type=jnp.float32)
    base_output_share = lax.psum_scatter(
        partial_base, ("tp", "sub"), scatter_dimension=1, tiled=True
    )
    return (base_output_share + adapter_row_output.astype(jnp.float32)).astype(jnp.bfloat16)


MESH_ID = pl.DeviceIdType.MESH
BOUNDS = (0, 4, 9, 14, 16)
CHUNKS = len(BOUNDS) - 1


def piece_of(chunk, depth):
    return BOUNDS[chunk] * depth // 16, (BOUNDS[chunk + 1] - BOUNDS[chunk]) * depth // 16


def page_in_turn(z, turn, n):
    if turn == 0:
        return z
    nearer = jnp.minimum(z, n - 1 - z)
    step = -((turn + 1) // 2) if turn % 2 else turn // 2
    beyond = jnp.where(z < n - 1 - z, z + (turn - nearer), z - (turn - nearer))
    return jnp.where(turn <= 2 * nearer, z + step, beyond)


def gather_kernel(
    n,
    adapters,
    tokens_hbm,
    base_hbm,
    down_hbm,
    up_hbm,
    index_hbm,
    slot_hbm,
    out_ref,
    index_ref,
    slot_ref,
    tok,
    basew,
    down_all,
    up_all,
    pack,
    pack_slot,
    place,
    pack_send,
    pack_back,
    part,
    picked,
    near_base,
    far_base,
    shrink_send,
    near_shrink,
    far_send,
    far_shrink,
    load_sem,
    right_sem,
    left_sem,
    recv_sem,
    pack_send_sem,
    pack_recv_sem,
    sum_send_sem,
    sum_recv_sem,
):
    z, t, s = lax.axis_index("page"), lax.axis_index("tp"), lax.axis_index("sub")
    rows, depth = tok.shape
    rank = ADAPTER_RANK
    group = down_all.shape[2] // rank

    loads = [
        pltpu.make_async_copy(down_hbm, down_all.at[z], load_sem.at[0]),
        pltpu.make_async_copy(up_hbm, up_all.at[z], load_sem.at[1]),
        pltpu.make_async_copy(tokens_hbm, tok, load_sem.at[2]),
        pltpu.make_async_copy(base_hbm, basew, load_sem.at[3]),
        pltpu.make_async_copy(index_hbm, index_ref, load_sem.at[4]),
        pltpu.make_async_copy(slot_hbm, slot_ref, load_sem.at[5]),
    ]
    for load in loads:
        load.start()

    barrier = pltpu.get_barrier_semaphore()
    pl.semaphore_signal(barrier, inc=1, device_id={"tp": 1 - t}, device_id_type=MESH_ID)
    pl.semaphore_signal(barrier, inc=1, device_id={"sub": 1 - s}, device_id_type=MESH_ID)

    @pl.when(z > 0)
    def _():
        pl.semaphore_signal(barrier, inc=1, device_id={"page": z - 1}, device_id_type=MESH_ID)

    @pl.when(z < n - 1)
    def _():
        pl.semaphore_signal(barrier, inc=1, device_id={"page": z + 1}, device_id_type=MESH_ID)

    pl.semaphore_wait(barrier, 2 + (z > 0).astype(jnp.int32) + (z < n - 1).astype(jnp.int32))

    end = (z == 0) | (z == n - 1)
    helped = jnp.where(z == 1, 0, n - 1)
    helper = jnp.where(z == 0, 1, n - 2)
    opposite = n - 1 - z
    outer = jnp.where(z == 1, 0, n - 1)

    def hop(page, chunk, to, sems, own=False):
        if chunk < CHUNKS:
            span = pl.ds(*piece_of(chunk, depth))
            ref = down_all.at[page, span, :]
            src = down_hbm.at[span, :] if own else ref
        else:
            ref = up_all.at[page]
            src = up_hbm if own else ref
        return pltpu.make_async_remote_copy(
            src_ref=src,
            dst_ref=ref,
            send_sem=sems.at[page, chunk],
            recv_sem=recv_sem.at[page, chunk],
            device_id={"page": to},
            device_id_type=MESH_ID,
        )

    def goes_right(page, chunk):
        goes = (page <= z) & (z < n - 1)
        return goes & ~((z == n - 2) & (page == 0)) if chunk < CHUNKS else goes

    def goes_left(page, chunk):
        goes = (page >= z) & (z > 0)
        return goes & ~((z == 1) & (page == n - 1)) if chunk < CHUNKS else goes

    def send_on(page, chunk, own=False):
        late = own and chunk == CHUNKS - 1

        @pl.when(goes_right(page, chunk) & ~((z == 1) & late))
        def _():
            hop(page, chunk, z + 1, right_sem, own).start()

        @pl.when(goes_left(page, chunk) & ~((z == n - 2) & late))
        def _():
            hop(page, chunk, z - 1, left_sem, own).start()

    for chunk in (CHUNKS, *range(CHUNKS)):
        send_on(z, chunk, own=True)

    def pack_copy(k, to):
        ref = (pack, pack_slot)[k]
        return pltpu.make_async_remote_copy(
            src_ref=ref,
            dst_ref=ref,
            send_sem=pack_send_sem.at[k],
            recv_sem=pack_recv_sem.at[k],
            device_id={"page": to},
            device_id_type=MESH_ID,
        )

    def pack_return(to):
        return pltpu.make_async_remote_copy(
            src_ref=pack_send,
            dst_ref=pack_back,
            send_sem=pack_send_sem.at[2],
            recv_sem=pack_recv_sem.at[2],
            device_id={"page": to},
            device_id_type=MESH_ID,
        )

    loads[4].wait()
    loads[5].wait()
    slot_row = jnp.zeros(index_ref.shape, jnp.float32)
    for a in range(adapters):
        slot_row = jnp.where(index_ref[...] == a, slot_ref[a].astype(jnp.float32), slot_row)
    slot = jnp.transpose(jnp.broadcast_to(slot_row, (128, rows)))
    lane = lax.broadcasted_iota(jnp.int32, (rows, 128), 1)
    half = (lane // rank).astype(jnp.float32)
    loads[2].wait()
    cap = pack.shape[0]

    @pl.when(end)
    def _():
        lowest = (opposite * group).astype(jnp.float32)
        mine = (slot_row >= lowest) & (slot_row < lowest + float(group))
        marks = jnp.broadcast_to(jnp.where(mine, 1.0, 0.0), (16, rows)).astype(jnp.bfloat16)
        earlier = lax.broadcasted_iota(jnp.int32, (rows, rows), 0) < lax.broadcasted_iota(
            jnp.int32, (rows, rows), 1
        )
        position = jnp.dot(
            marks,
            jnp.where(earlier, 1.0, 0.0).astype(jnp.bfloat16),
            preferred_element_type=jnp.float32,
        )[:1]
        target = jnp.where(mine, position, -1.0)
        spots = lax.broadcasted_iota(jnp.int32, (cap, rows), 0).astype(jnp.float32)
        place[...] = jnp.where(spots == target, 1.0, 0.0).astype(jnp.bfloat16)

        @pl.loop(0, depth // 512)
        def _(b):
            columns = pl.ds(pl.multiple_of(b * 512, 512), 512)
            pack[:, columns] = jnp.dot(
                place[...], tok[:, columns], preferred_element_type=jnp.float32
            ).astype(jnp.bfloat16)

        pack_slot[...] = lax.dot_general(
            jnp.broadcast_to(slot_row, (16, rows)).astype(jnp.bfloat16),
            place[...],
            (((1,), (1,)), ((), ())),
            preferred_element_type=jnp.float32,
        )[: pack_slot.shape[0]]
        for k in range(2):
            pack_copy(k, helper).start()

    loads[3].wait()
    blocks, width = part.shape[0], part.shape[2]

    @pl.loop(0, blocks)
    def _(b):
        columns = pl.ds(pl.multiple_of(b * width, width), width)
        part[b] = jnp.dot(tok[...], basew[:, columns], preferred_element_type=jnp.float32)

    def to_sibling(k):
        return pltpu.make_async_remote_copy(
            src_ref=part.at[2 * k + 1 - s],
            dst_ref=near_base.at[k],
            send_sem=sum_send_sem.at[k],
            recv_sem=sum_recv_sem.at[k],
            device_id={"sub": 1 - s},
            device_id_type=MESH_ID,
        )

    base_far = pltpu.make_async_remote_copy(
        src_ref=part.at[2 * (1 - t) + s],
        dst_ref=far_base,
        send_sem=sum_send_sem.at[2],
        recv_sem=sum_recv_sem.at[2],
        device_id={"tp": 1 - t},
        device_id_type=MESH_ID,
    )
    for k in range(2):
        to_sibling(k).start()

    def pick(page, product, slot, half):
        first = (page * group).astype(jnp.float32) + half
        total = jnp.zeros(slot.shape, jnp.float32)
        for g in range(group * rank // 128):
            hit = slot == first + float(g * (128 // rank))
            total += jnp.where(hit, product[:, g * 128 : g * 128 + 128], 0.0)
        return total

    def product_of(ref, page, chunk):
        return jnp.dot(
            ref[:, pl.ds(*piece_of(chunk, depth))],
            down_all[page, pl.ds(*piece_of(chunk, depth)), :],
            preferred_element_type=jnp.float32,
        )

    def take_piece(page, chunk):
        picked[...] += pick(page, product_of(tok, page, chunk), slot, half)

    def pass_on(page, chunk):
        hop(page, chunk, z, left_sem).wait_recv()
        send_on(page, chunk)

    loads[0].wait()
    loads[1].wait()
    picked[...] = jnp.zeros_like(picked)
    for chunk in range(CHUNKS):
        take_piece(z, chunk)
    for k in range(2):
        to_sibling(k).wait_recv()
    part[2 * (1 - t) + s] += near_base[1 - t]
    base_far.start()
    last = page_in_turn(z, n - 1, n)
    between = [page_in_turn(z, turn, n) for turn in range(1, n - 1)]
    for page in between:
        pass_on(page, CHUNKS)

    @pl.when(~end)
    def _():
        for chunk in range(CHUNKS - 1):
            pass_on(outer, chunk)
            pass_on(opposite, chunk)
            take_piece(outer, chunk)
            take_piece(opposite, chunk)
        pass_on(outer, CHUNKS - 1)

        @pl.when(z == 1)
        def _():
            hop(z, CHUNKS - 1, z + 1, right_sem, True).start()

        @pl.when(z == n - 2)
        def _():
            hop(z, CHUNKS - 1, z - 1, left_sem, True).start()

        take_piece(outer, CHUNKS - 1)

    @pl.when(end)
    def _():
        for page in between:
            for chunk in range(CHUNKS):
                pass_on(page, chunk)
                take_piece(page, chunk)

    pass_on(last, CHUNKS)

    @pl.when(~end)
    def _():
        for k in range(2):
            pack_copy(k, z).wait_recv()
        their_slot = jnp.transpose(jnp.broadcast_to(pack_slot[:1], (128, cap)))
        theirs = jnp.zeros((cap, 128), jnp.float32)
        for chunk in range(CHUNKS):
            pass_on(last, chunk)
            theirs += pick(last, product_of(pack, last, chunk), their_slot, half[:cap])
            if chunk < CHUNKS - 1:
                take_piece(last, chunk)
        theirs += pltpu.roll(theirs, rank, 1)
        pack_send[...] = jnp.where(
            lane[: cap // 2] < rank, theirs[: cap // 2], theirs[cap // 2 :]
        ).astype(jnp.bfloat16)
        pack_return(helped).start()
        pass_on(opposite, CHUNKS - 1)
        take_piece(last, CHUNKS - 1)
        take_piece(opposite, CHUNKS - 1)

    @pl.when(end)
    def _():
        pack_return(z).wait_recv()
        back = pack_back[...].astype(jnp.float32)
        back = jnp.concatenate([back, pltpu.roll(back, rank, 1)], axis=0)
        back = jnp.where(lane[:cap] < rank, back, 0.0).astype(jnp.bfloat16)
        picked[...] += lax.dot_general(
            place[...], back, (((0,), (0,)), ((), ())), preferred_element_type=jnp.float32
        )

    folded = picked[...] + pltpu.roll(picked[...], rank, 1)
    low = lane[: rows // 2] < rank
    shrink_send[...] = jnp.where(low, folded[: rows // 2], folded[rows // 2 :])
    near = pltpu.make_async_remote_copy(
        src_ref=shrink_send,
        dst_ref=near_shrink,
        send_sem=sum_send_sem.at[3],
        recv_sem=sum_recv_sem.at[3],
        device_id={"sub": 1 - s},
        device_id_type=MESH_ID,
    )
    near.start()
    near.wait_recv()
    chip_sum = shrink_send[...] + near_shrink[...]
    far_send[...] = chip_sum.astype(jnp.bfloat16)
    far = pltpu.make_async_remote_copy(
        src_ref=far_send,
        dst_ref=far_shrink,
        send_sem=sum_send_sem.at[4],
        recv_sem=sum_recv_sem.at[4],
        device_id={"tp": 1 - t},
        device_id_type=MESH_ID,
    )
    far.start()
    base_far.wait_recv()
    part[2 * t + s] += near_base[t] + far_base[...]
    far.wait_recv()
    both = chip_sum + far_shrink[...].astype(jnp.float32)
    both = both.astype(jnp.bfloat16).astype(jnp.float32)
    turned = pltpu.roll(both, rank, 1)
    shrink = jnp.concatenate(
        [jnp.where(low, both, turned), jnp.where(low, turned, both)], axis=0
    )
    spread = jnp.concatenate(
        [
            jnp.where(slot == half + float(b * (128 // rank)), shrink, 0.0).astype(jnp.bfloat16)
            for b in range(n * group * rank // 128)
        ],
        axis=1,
    )
    expand = jnp.dot(
        spread,
        up_all[...].reshape(n * group * rank, up_all.shape[2]),
        preferred_element_type=jnp.float32,
    )
    lora = (expand * adapter_scale).astype(jnp.bfloat16).astype(jnp.float32)
    out_ref[...] = (part[2 * t + s] + lora).astype(jnp.bfloat16)

    for k in range(2):
        to_sibling(k).wait_send()
    base_far.wait_send()
    near.wait_send()
    far.wait_send()

    @pl.when(end)
    def _():
        for k in range(2):
            pack_copy(k, helper).wait_send()

    @pl.when(~end)
    def _():
        pack_return(helped).wait_send()

    for turn in range(n):
        page = page_in_turn(z, turn, n)
        for chunk in range(CHUNKS + 1):

            @pl.when(goes_right(page, chunk))
            def _():
                hop(page, chunk, z + 1, right_sem, turn == 0).wait_send()

            @pl.when(goes_left(page, chunk))
            def _():
                hop(page, chunk, z - 1, left_sem, turn == 0).wait_send()


def gather_weights_body(
    tokens,
    base_value_weight,
    adapter_down_weight,
    adapter_up_weight,
    row_adapter_index,
    adapter_storage_slot,
):
    n = lax.axis_size("page")
    rows, depth = tokens.shape
    width = adapter_down_weight.shape[1]
    share = adapter_up_weight.shape[1]
    blocks = base_value_weight.shape[1] // share
    adapters = adapter_storage_slot.shape[0]
    cap = rows // 2
    f32, bf16 = jnp.float32, jnp.bfloat16
    return pl.pallas_call(
        functools.partial(gather_kernel, n, adapters),
        out_shape=jax.ShapeDtypeStruct((rows, share), bf16),
        in_specs=[pl.BlockSpec(memory_space=pltpu.HBM)] * 6,
        out_specs=pl.BlockSpec(memory_space=pltpu.VMEM),
        scratch_shapes=[
            pltpu.VMEM((1, rows), jnp.int32),
            pltpu.SMEM((adapters,), jnp.int32),
            pltpu.VMEM((rows, depth), bf16),
            pltpu.VMEM(base_value_weight.shape, bf16),
            pltpu.VMEM((n, depth, width), bf16),
            pltpu.VMEM((n, width, share), bf16),
            pltpu.VMEM((cap, depth), bf16),
            pltpu.VMEM((8, cap), f32),
            pltpu.VMEM((cap, rows), bf16),
            pltpu.VMEM((cap // 2, 128), bf16),
            pltpu.VMEM((cap // 2, 128), bf16),
            pltpu.VMEM((blocks, rows, share), f32),
            pltpu.VMEM((rows, 128), f32),
            pltpu.VMEM((2, rows, share), f32),
            pltpu.VMEM((rows, share), f32),
            pltpu.VMEM((rows // 2, 128), f32),
            pltpu.VMEM((rows // 2, 128), f32),
            pltpu.VMEM((rows // 2, 128), bf16),
            pltpu.VMEM((rows // 2, 128), bf16),
            pltpu.SemaphoreType.DMA((6,)),
            pltpu.SemaphoreType.DMA((n, CHUNKS + 1)),
            pltpu.SemaphoreType.DMA((n, CHUNKS + 1)),
            pltpu.SemaphoreType.DMA((n, CHUNKS + 1)),
            pltpu.SemaphoreType.DMA((3,)),
            pltpu.SemaphoreType.DMA((3,)),
            pltpu.SemaphoreType.DMA((5,)),
            pltpu.SemaphoreType.DMA((5,)),
        ],
        compiler_params=pltpu.CompilerParams(
            collective_id=0, has_side_effects=True, vmem_limit_bytes=60 * 1024 * 1024
        ),
    )(
        tokens,
        base_value_weight,
        adapter_down_weight,
        adapter_up_weight,
        row_adapter_index.reshape(1, rows),
        adapter_storage_slot,
    )


def solution(mesh):
    sizes = mesh.shape
    gathers = sizes["page"] == 4 and sizes["tp"] == 2 and sizes["sub"] == 2
    return jax.shard_map(
        gather_weights_body if gathers else exchange_rows_body,
        mesh=mesh,
        in_specs=(
            P(("grp", "page"), ("tp", "sub")),
            P(("tp", "sub"), None),
            P(("grp", "tp", "sub"), "page"),
            P(("grp", "page"), ("tp", "sub")),
            P(("grp", "page")),
            P("grp"),
        ),
        out_specs=P(("grp", "page"), ("tp", "sub")),
        check_vma=False,
    )
```

```python
import functools

import jax
import jax.numpy as jnp
from jax import lax
from jax.experimental import pallas as pl
from jax.experimental.pallas import tpu as pltpu
from jax.sharding import PartitionSpec as P

ADAPTER_RANK = 64


adapter_scale = 0.5


def rank_within(labels, count):
    onehot = (labels[:, None] == jnp.arange(count, dtype=jnp.int32)[None, :]).astype(jnp.int32)
    before = jnp.cumsum(onehot, axis=0) - onehot
    return jnp.sum(before * onehot, axis=1)


def build_device_worker(down_cols, up_weight_rows):
    width = down_cols.shape[1]
    row_grouping = width // ADAPTER_RANK
    column_group = jnp.arange(width, dtype=jnp.int32) // ADAPTER_RANK

    def owner_work(pair):
        rows, marks = pair
        sources = marks.shape[0]
        count = marks.shape[1]
        feat = rows.shape[2]
        flat_rows = rows.reshape(sources * count, feat)
        owner_ids = marks.reshape(sources * count).astype(jnp.int32)
        select = owner_ids[:, None] == column_group[None, :]
        partial_all = jnp.dot(flat_rows, down_cols, preferred_element_type=jnp.float32)
        picked = (
            jnp.where(select, partial_all, 0.0)
            .reshape(sources * count, row_grouping, ADAPTER_RANK)
            .sum(axis=1)
        )
        shrink_rank = lax.psum(picked, ("tp", "sub")).astype(jnp.bfloat16)
        spread_rows = jnp.where(
            select, jnp.tile(shrink_rank, (1, row_grouping)), jnp.zeros((), jnp.bfloat16)
        )
        expand_rank = (
            jnp.dot(spread_rows, up_weight_rows, preferred_element_type=jnp.float32) * adapter_scale
        )
        return expand_rank.astype(jnp.bfloat16).reshape(sources, count, expand_rank.shape[1])

    return owner_work


def pack_boxes(tokens, flattened, marks, adapter_pages, slot_capacity):
    feat = tokens.shape[1]
    outbox = (
        jnp.zeros((adapter_pages * slot_capacity, feat), jnp.bfloat16).at[flattened].set(tokens)
    )
    labels = (
        jnp.full((adapter_pages * slot_capacity,), -1.0, jnp.bfloat16)
        .at[flattened]
        .set(marks.astype(jnp.bfloat16))
    )
    return (
        outbox.reshape(adapter_pages, slot_capacity, feat),
        labels.reshape(adapter_pages, slot_capacity),
    )


def exchange_rows_body(
    tokens,
    base_value_weight,
    adapter_down_weight,
    adapter_up_weight,
    row_adapter_index,
    adapter_storage_slot,
):
    adapter_pages = lax.axis_size("page")
    row_dev = tokens.shape[0]
    slot_capacity = min(4 * row_dev // adapter_pages, row_dev // 2)
    row_grouping = adapter_down_weight.shape[1] // ADAPTER_RANK
    hits = (
        row_adapter_index[:, None]
        == jnp.arange(adapter_storage_slot.shape[0], dtype=jnp.int32)[None, :]
    )
    storage_position = jnp.sum(jnp.where(hits, adapter_storage_slot[None, :], 0), axis=1)
    target = storage_position // row_grouping
    within = storage_position % row_grouping
    position = rank_within(target, adapter_pages)
    flattened = target * slot_capacity + position
    outbox, labels = pack_boxes(tokens, flattened, within, adapter_pages, slot_capacity)
    device_worker = build_device_worker(adapter_down_weight, adapter_up_weight)
    finished = device_worker(
        (
            lax.all_to_all(outbox, "page", split_axis=0, concat_axis=0, tiled=True),
            lax.all_to_all(labels, "page", split_axis=0, concat_axis=0, tiled=True),
        )
    )
    returned_output = lax.all_to_all(finished, "page", split_axis=0, concat_axis=0, tiled=True)
    adapter_row_output = returned_output.reshape(
        adapter_pages * slot_capacity, returned_output.shape[2]
    )[flattened]
    partial_base = jnp.dot(tokens, base_value_weight, preferred_element_type=jnp.float32)
    base_output_share = lax.psum_scatter(
        partial_base, ("tp", "sub"), scatter_dimension=1, tiled=True
    )
    return (base_output_share + adapter_row_output.astype(jnp.float32)).astype(jnp.bfloat16)


MESH_ID = pl.DeviceIdType.MESH
CHUNKS = 4


def page_in_turn(z, turn, n):
    if turn == 0:
        return z
    nearer = jnp.minimum(z, n - 1 - z)
    step = -((turn + 1) // 2) if turn % 2 else turn // 2
    beyond = jnp.where(z < n - 1 - z, z + (turn - nearer), z - (turn - nearer))
    return jnp.where(turn <= 2 * nearer, z + step, beyond)


def gather_kernel(
    n,
    adapters,
    tokens_hbm,
    base_hbm,
    down_hbm,
    up_hbm,
    index_hbm,
    slot_hbm,
    lora_ref,
    base_out,
    index_ref,
    slot_ref,
    tok,
    basew,
    down_all,
    up_all,
    pack,
    pack_slot,
    place,
    pack_send,
    pack_back,
    part,
    picked,
    near_base,
    far_base,
    shrink_send,
    near_shrink,
    far_send,
    far_shrink,
    load_sem,
    right_sem,
    left_sem,
    recv_sem,
    pack_send_sem,
    pack_recv_sem,
    sum_send_sem,
    sum_recv_sem,
):
    z, t, s = lax.axis_index("page"), lax.axis_index("tp"), lax.axis_index("sub")
    rows, depth = tok.shape
    rank = ADAPTER_RANK
    group = down_all.shape[2] // rank
    piece = depth // CHUNKS

    loads = [
        pltpu.make_async_copy(down_hbm, down_all.at[z], load_sem.at[0]),
        pltpu.make_async_copy(up_hbm, up_all.at[z], load_sem.at[1]),
        pltpu.make_async_copy(tokens_hbm, tok, load_sem.at[2]),
        pltpu.make_async_copy(base_hbm, basew, load_sem.at[3]),
        pltpu.make_async_copy(index_hbm, index_ref, load_sem.at[4]),
        pltpu.make_async_copy(slot_hbm, slot_ref, load_sem.at[5]),
    ]
    for load in loads:
        load.start()

    barrier = pltpu.get_barrier_semaphore()
    pl.semaphore_signal(barrier, inc=1, device_id={"tp": 1 - t}, device_id_type=MESH_ID)
    pl.semaphore_signal(barrier, inc=1, device_id={"sub": 1 - s}, device_id_type=MESH_ID)

    @pl.when(z > 0)
    def _():
        pl.semaphore_signal(barrier, inc=1, device_id={"page": z - 1}, device_id_type=MESH_ID)

    @pl.when(z < n - 1)
    def _():
        pl.semaphore_signal(barrier, inc=1, device_id={"page": z + 1}, device_id_type=MESH_ID)

    pl.semaphore_wait(barrier, 2 + (z > 0).astype(jnp.int32) + (z < n - 1).astype(jnp.int32))

    end = (z == 0) | (z == n - 1)
    helped = jnp.where(z == 1, 0, n - 1)
    helper = jnp.where(z == 0, 1, n - 2)
    opposite = n - 1 - z

    def hop(page, chunk, to, sems, own=False):
        if chunk < CHUNKS:
            ref = down_all.at[page, pl.ds(chunk * piece, piece), :]
            src = down_hbm.at[pl.ds(chunk * piece, piece), :] if own else ref
        else:
            ref = up_all.at[page]
            src = up_hbm if own else ref
        return pltpu.make_async_remote_copy(
            src_ref=src,
            dst_ref=ref,
            send_sem=sems.at[page, chunk],
            recv_sem=recv_sem.at[page, chunk],
            device_id={"page": to},
            device_id_type=MESH_ID,
        )

    def goes_right(page, chunk):
        goes = (page <= z) & (z < n - 1)
        return goes & ~((z == n - 2) & (page == 0)) if chunk < CHUNKS else goes

    def goes_left(page, chunk):
        goes = (page >= z) & (z > 0)
        return goes & ~((z == 1) & (page == n - 1)) if chunk < CHUNKS else goes

    def send_on(page, chunk, own=False):
        @pl.when(goes_right(page, chunk))
        def _():
            hop(page, chunk, z + 1, right_sem, own).start()

        @pl.when(goes_left(page, chunk))
        def _():
            hop(page, chunk, z - 1, left_sem, own).start()

    for chunk in (CHUNKS, *range(CHUNKS)):
        send_on(z, chunk, own=True)

    def pack_copy(k, to):
        ref = (pack, pack_slot)[k]
        return pltpu.make_async_remote_copy(
            src_ref=ref,
            dst_ref=ref,
            send_sem=pack_send_sem.at[k],
            recv_sem=pack_recv_sem.at[k],
            device_id={"page": to},
            device_id_type=MESH_ID,
        )

    def pack_return(to):
        return pltpu.make_async_remote_copy(
            src_ref=pack_send,
            dst_ref=pack_back,
            send_sem=pack_send_sem.at[2],
            recv_sem=pack_recv_sem.at[2],
            device_id={"page": to},
            device_id_type=MESH_ID,
        )

    loads[4].wait()
    loads[5].wait()
    slot_row = jnp.zeros(index_ref.shape, jnp.float32)
    for a in range(adapters):
        slot_row = jnp.where(index_ref[...] == a, slot_ref[a].astype(jnp.float32), slot_row)
    slot = jnp.transpose(jnp.broadcast_to(slot_row, (128, rows)))
    lane = lax.broadcasted_iota(jnp.int32, (rows, 128), 1)
    half = (lane // rank).astype(jnp.float32)
    loads[2].wait()
    cap = pack.shape[0]

    @pl.when(end)
    def _():
        lowest = (opposite * group).astype(jnp.float32)
        mine = (slot_row >= lowest) & (slot_row < lowest + float(group))
        marks = jnp.broadcast_to(jnp.where(mine, 1.0, 0.0), (16, rows)).astype(jnp.bfloat16)
        earlier = lax.broadcasted_iota(jnp.int32, (rows, rows), 0) < lax.broadcasted_iota(
            jnp.int32, (rows, rows), 1
        )
        position = jnp.dot(
            marks,
            jnp.where(earlier, 1.0, 0.0).astype(jnp.bfloat16),
            preferred_element_type=jnp.float32,
        )[:1]
        target = jnp.where(mine, position, -1.0)
        spots = lax.broadcasted_iota(jnp.int32, (cap, rows), 0).astype(jnp.float32)
        place[...] = jnp.where(spots == target, 1.0, 0.0).astype(jnp.bfloat16)

        @pl.loop(0, depth // 512)
        def _(b):
            columns = pl.ds(pl.multiple_of(b * 512, 512), 512)
            pack[:, columns] = jnp.dot(
                place[...], tok[:, columns], preferred_element_type=jnp.float32
            ).astype(jnp.bfloat16)

        pack_slot[...] = lax.dot_general(
            jnp.broadcast_to(slot_row, (16, rows)).astype(jnp.bfloat16),
            place[...],
            (((1,), (1,)), ((), ())),
            preferred_element_type=jnp.float32,
        )[: pack_slot.shape[0]]
        for k in range(2):
            pack_copy(k, helper).start()

    loads[3].wait()
    blocks, width = part.shape[0], part.shape[2]

    @pl.loop(0, blocks)
    def _(b):
        columns = pl.ds(pl.multiple_of(b * width, width), width)
        part[b] = jnp.dot(tok[...], basew[:, columns], preferred_element_type=jnp.float32)

    def to_sibling(k):
        return pltpu.make_async_remote_copy(
            src_ref=part.at[2 * k + 1 - s],
            dst_ref=near_base.at[k],
            send_sem=sum_send_sem.at[k],
            recv_sem=sum_recv_sem.at[k],
            device_id={"sub": 1 - s},
            device_id_type=MESH_ID,
        )

    base_far = pltpu.make_async_remote_copy(
        src_ref=part.at[2 * (1 - t) + s],
        dst_ref=far_base,
        send_sem=sum_send_sem.at[2],
        recv_sem=sum_recv_sem.at[2],
        device_id={"tp": 1 - t},
        device_id_type=MESH_ID,
    )
    for k in range(2):
        to_sibling(k).start()

    def pick(page, product, slot, half):
        first = (page * group).astype(jnp.float32) + half
        total = jnp.zeros(slot.shape, jnp.float32)
        for g in range(group * rank // 128):
            hit = slot == first + float(g * (128 // rank))
            total += jnp.where(hit, product[:, g * 128 : g * 128 + 128], 0.0)
        return total

    def product_of(ref, page, chunk):
        return jnp.dot(
            ref[:, chunk * piece : chunk * piece + piece],
            down_all[page, pl.ds(chunk * piece, piece), :],
            preferred_element_type=jnp.float32,
        )

    def take_piece(page, chunk):
        picked[...] += pick(page, product_of(tok, page, chunk), slot, half)

    def pass_on(page, chunk):
        hop(page, chunk, z, left_sem).wait_recv()
        send_on(page, chunk)

    loads[0].wait()
    loads[1].wait()
    picked[...] = jnp.zeros_like(picked)
    for chunk in range(CHUNKS):
        take_piece(z, chunk)
    for k in range(2):
        to_sibling(k).wait_recv()
    part[2 * (1 - t) + s] += near_base[1 - t]
    base_far.start()
    last = page_in_turn(z, n - 1, n)
    between = [page_in_turn(z, turn, n) for turn in range(1, n - 1)]
    for page in between:
        pass_on(page, CHUNKS)

    @pl.when(~end)
    def _():
        for chunk in range(CHUNKS):
            for page in between:
                pass_on(page, chunk)
            for page in between:
                take_piece(page, chunk)

    @pl.when(end)
    def _():
        for page in between:
            for chunk in range(CHUNKS):
                pass_on(page, chunk)
                take_piece(page, chunk)

    pass_on(last, CHUNKS)

    @pl.when(~end)
    def _():
        for k in range(2):
            pack_copy(k, z).wait_recv()
        their_slot = jnp.transpose(jnp.broadcast_to(pack_slot[:1], (128, cap)))
        theirs = jnp.zeros((cap, 128), jnp.float32)
        for chunk in range(CHUNKS):
            pass_on(last, chunk)
            theirs += pick(last, product_of(pack, last, chunk), their_slot, half[:cap])
            if chunk < CHUNKS - 1:
                take_piece(last, chunk)
        theirs += pltpu.roll(theirs, rank, 1)
        pack_send[...] = jnp.where(
            lane[: cap // 2] < rank, theirs[: cap // 2], theirs[cap // 2 :]
        ).astype(jnp.bfloat16)
        pack_return(helped).start()
        take_piece(last, CHUNKS - 1)

    @pl.when(end)
    def _():
        pack_return(z).wait_recv()
        back = pack_back[...].astype(jnp.float32)
        back = jnp.concatenate([back, pltpu.roll(back, rank, 1)], axis=0)
        back = jnp.where(lane[:cap] < rank, back, 0.0).astype(jnp.bfloat16)
        picked[...] += lax.dot_general(
            place[...], back, (((0,), (0,)), ((), ())), preferred_element_type=jnp.float32
        )

    folded = picked[...] + pltpu.roll(picked[...], rank, 1)
    low = lane[: rows // 2] < rank
    shrink_send[...] = jnp.where(low, folded[: rows // 2], folded[rows // 2 :])
    near = pltpu.make_async_remote_copy(
        src_ref=shrink_send,
        dst_ref=near_shrink,
        send_sem=sum_send_sem.at[3],
        recv_sem=sum_recv_sem.at[3],
        device_id={"sub": 1 - s},
        device_id_type=MESH_ID,
    )
    near.start()
    near.wait_recv()
    chip_sum = shrink_send[...] + near_shrink[...]
    far_send[...] = chip_sum.astype(jnp.bfloat16)
    far = pltpu.make_async_remote_copy(
        src_ref=far_send,
        dst_ref=far_shrink,
        send_sem=sum_send_sem.at[4],
        recv_sem=sum_recv_sem.at[4],
        device_id={"tp": 1 - t},
        device_id_type=MESH_ID,
    )
    far.start()
    base_far.wait_recv()
    part[2 * t + s] += near_base[t] + far_base[...]
    store = pltpu.make_async_copy(part.at[2 * t + s], base_out, load_sem.at[6])
    store.start()
    far.wait_recv()
    both = chip_sum + far_shrink[...].astype(jnp.float32)
    both = both.astype(jnp.bfloat16).astype(jnp.float32)
    turned = pltpu.roll(both, rank, 1)
    shrink = jnp.concatenate(
        [jnp.where(low, both, turned), jnp.where(low, turned, both)], axis=0
    )
    spread = jnp.concatenate(
        [
            jnp.where(slot == half + float(b * (128 // rank)), shrink, 0.0).astype(jnp.bfloat16)
            for b in range(n * group * rank // 128)
        ],
        axis=1,
    )
    expand = jnp.dot(
        spread,
        up_all[...].reshape(n * group * rank, up_all.shape[2]),
        preferred_element_type=jnp.float32,
    )
    lora_ref[...] = (expand * adapter_scale).astype(jnp.bfloat16)
    store.wait()

    for k in range(2):
        to_sibling(k).wait_send()
    base_far.wait_send()
    near.wait_send()
    far.wait_send()

    @pl.when(end)
    def _():
        for k in range(2):
            pack_copy(k, helper).wait_send()

    @pl.when(~end)
    def _():
        pack_return(helped).wait_send()

    for turn in range(n):
        page = page_in_turn(z, turn, n)
        for chunk in range(CHUNKS + 1):

            @pl.when(goes_right(page, chunk))
            def _():
                hop(page, chunk, z + 1, right_sem, turn == 0).wait_send()

            @pl.when(goes_left(page, chunk))
            def _():
                hop(page, chunk, z - 1, left_sem, turn == 0).wait_send()


def gather_weights_body(
    tokens,
    base_value_weight,
    adapter_down_weight,
    adapter_up_weight,
    row_adapter_index,
    adapter_storage_slot,
):
    n = lax.axis_size("page")
    rows, depth = tokens.shape
    width = adapter_down_weight.shape[1]
    share = adapter_up_weight.shape[1]
    blocks = base_value_weight.shape[1] // share
    adapters = adapter_storage_slot.shape[0]
    cap = rows // 2
    f32, bf16 = jnp.float32, jnp.bfloat16
    lora, base = pl.pallas_call(
        functools.partial(gather_kernel, n, adapters),
        out_shape=(
            jax.ShapeDtypeStruct((rows, share), bf16),
            jax.ShapeDtypeStruct((rows, share), f32),
        ),
        in_specs=[pl.BlockSpec(memory_space=pltpu.HBM)] * 6,
        out_specs=(
            pl.BlockSpec(memory_space=pltpu.VMEM),
            pl.BlockSpec(memory_space=pltpu.HBM),
        ),
        scratch_shapes=[
            pltpu.VMEM((1, rows), jnp.int32),
            pltpu.SMEM((adapters,), jnp.int32),
            pltpu.VMEM((rows, depth), bf16),
            pltpu.VMEM(base_value_weight.shape, bf16),
            pltpu.VMEM((n, depth, width), bf16),
            pltpu.VMEM((n, width, share), bf16),
            pltpu.VMEM((cap, depth), bf16),
            pltpu.VMEM((8, cap), f32),
            pltpu.VMEM((cap, rows), bf16),
            pltpu.VMEM((cap // 2, 128), bf16),
            pltpu.VMEM((cap // 2, 128), bf16),
            pltpu.VMEM((blocks, rows, share), f32),
            pltpu.VMEM((rows, 128), f32),
            pltpu.VMEM((2, rows, share), f32),
            pltpu.VMEM((rows, share), f32),
            pltpu.VMEM((rows // 2, 128), f32),
            pltpu.VMEM((rows // 2, 128), f32),
            pltpu.VMEM((rows // 2, 128), bf16),
            pltpu.VMEM((rows // 2, 128), bf16),
            pltpu.SemaphoreType.DMA((7,)),
            pltpu.SemaphoreType.DMA((n, CHUNKS + 1)),
            pltpu.SemaphoreType.DMA((n, CHUNKS + 1)),
            pltpu.SemaphoreType.DMA((n, CHUNKS + 1)),
            pltpu.SemaphoreType.DMA((3,)),
            pltpu.SemaphoreType.DMA((3,)),
            pltpu.SemaphoreType.DMA((5,)),
            pltpu.SemaphoreType.DMA((5,)),
        ],
        compiler_params=pltpu.CompilerParams(
            collective_id=0, has_side_effects=True, vmem_limit_bytes=60 * 1024 * 1024
        ),
    )(
        tokens,
        base_value_weight,
        adapter_down_weight,
        adapter_up_weight,
        row_adapter_index.reshape(1, rows),
        adapter_storage_slot,
    )
    return (base + lora.astype(f32)).astype(bf16)


def solution(mesh):
    sizes = mesh.shape
    gathers = sizes["page"] == 4 and sizes["tp"] == 2 and sizes["sub"] == 2
    return jax.shard_map(
        gather_weights_body if gathers else exchange_rows_body,
        mesh=mesh,
        in_specs=(
            P(("grp", "page"), ("tp", "sub")),
            P(("tp", "sub"), None),
            P(("grp", "tp", "sub"), "page"),
            P(("grp", "page"), ("tp", "sub")),
            P(("grp", "page")),
            P("grp"),
        ),
        out_specs=P(("grp", "page"), ("tp", "sub")),
        check_vma=False,
    )
```
